256 devices in a mesh: ctx: 32 (over z_hi, y, core), mp: 8 (over x, z_lo).
Axes of the slice: x: 4, y: 4, z: 8 (z_hi: 4, z_lo: 2; z = z_hi * 2 + z_lo), core: 2. Of those that a mesh axis runs over, the one named last changes fastest.
Arguments:
- query_rows: bfloat16 [5120, 5120], P('ctx', 'mp'), may hold values from -42 to 42
- key_rows: bfloat16 [5120, 1024], P('ctx', 'mp'), may hold values from -42 to 42
- value_matrix: bfloat16 [5120, 1024], P('ctx', 'mp'), may hold values from -6 to 6
- cotangent: bfloat16 [5120, 5120], P('ctx', 'mp'), may hold values from -6 to 6
- frozen_out: bfloat16 [5120, 5120], P('mp'), may hold values from -0.078125 to 0.078125
- adapter_down: bfloat16 [5120, 64], P('mp'), may hold values from -0.078125 to 0.078125
- adapter_up: bfloat16 [64, 5120], replicated, may hold values from -0.0390625 to 0.0390625
- doc_lengths: int32 [4], replicated, may hold values from 1 to 2560, 5120 in all
Outputs:
- query_grads: bfloat16 [5120, 5120], P('ctx', 'mp')
- key_gradient: bfloat16 [5120, 1024], P('ctx', 'mp')
- value_gradient: bfloat16 [5120, 1024], P('ctx', 'mp')
- down_grad: float32 [5120, 64], P('mp')
- up_grad: float32 [64, 5120], P(None, 'mp')
The draws below stay inside these ranges and needn't reach their ends.
Inputs may be any that keep to these rules, and one draw needn't show every extreme that they name: `doc_lengths`: the 4 documents fill the window in order, their lengths sum to 5120, and the longest is exactly half of 5120 long.
All inputs are finite; a program needn't handle non-finite values.
Results may differ from the reference program's by a relative error of at most 0.04.
Values may be sent and summed in bfloat16 or wider, within the bound.
A program may use at most 64 MiB of HBM per device.

```python
import math
import jax
import jax.numpy as jnp
import numpy as np
from jax import lax

D = 5120
QUERY_HEADS = 40
KEY_VALUE_HEADS = 8
HEAD_SIZE = 128
R = 64
DOCS = 4
WINDOW_TOKENS = 5120


def paired_rows(key):
    base_scale = 2.0
    query_start = base_scale * jax.random.truncated_normal(jax.random.fold_in(key, 101), -6.0, 6.0, (WINDOW_TOKENS, QUERY_HEADS, HEAD_SIZE), jnp.float32)
    key_start = base_scale * jax.random.truncated_normal(jax.random.fold_in(key, 102), -6.0, 6.0, (WINDOW_TOKENS, KEY_VALUE_HEADS, HEAD_SIZE), jnp.float32)
    query_matrix = query_start
    key_result = key_start
    return (query_matrix.reshape(WINDOW_TOKENS, QUERY_HEADS * HEAD_SIZE), key_result.reshape(WINDOW_TOKENS, KEY_VALUE_HEADS * HEAD_SIZE))


def draw_query_rows(key, part):
    query_matrix, key_result = paired_rows(key)
    return query_matrix.astype(jnp.bfloat16)


def draw_key_rows(key, part):
    query_matrix, key_result = paired_rows(key)
    return key_result.astype(jnp.bfloat16)


def shard_levels(stream_key, dims, pieces, low, high):
    factor_of, own = 1.0, jax.random.fold_in(stream_key, 6)
    for position, shards_of in pieces:
        steps = jnp.exp(jax.random.uniform(jax.random.fold_in(own, position), (shards_of,), jnp.float32, low / len(pieces), high / len(pieces)))
        factor_of = factor_of * jnp.repeat(steps, dims[position] // shards_of).reshape([-1 if axis == position else 1 for axis in range(len(dims))])
    return factor_of


def split_up(number_of, total, bound, slope):
    portions = [(1 << 20) // math.isqrt(rank ** slope) + 1 for rank in range(2, number_of + 1)]
    rest, counts = total - bound - (number_of - 1), [1] * (number_of - 1)
    while rest > 0:
        candidates = [i for i in range(number_of - 1) if counts[i] < bound]
        mass, remaining = sum([portions[i] for i in candidates]), rest
        for i in candidates:
            more = min(bound - counts[i], max(1, remaining * portions[i] // mass), rest)
            counts[i] = counts[i] + more
            rest = rest - more
    return np.array([bound] + counts)


def uneven_parts(own_key, count, total, limit, lean):
    if count == 2:
        one = jax.random.randint(own_key, (), max(1, total - limit), min(limit, total - 1) + 1)
        return jnp.stack([one, total - one])
    tallies = jnp.asarray(split_up(count, total, limit, lean), jnp.int32)
    pairs = (count - 1) // 2
    source_of, taker = tallies[1:1 + 2 * pairs:2], tallies[2:2 + 2 * pairs:2]
    room = jnp.minimum(source_of - 1, limit - taker)
    moved = jax.random.randint(jax.random.fold_in(own_key, 1), (pairs,), 0, 1 << 20) % (room + 1)
    tallies = tallies.at[1:1 + 2 * pairs:2].set(source_of - moved).at[2:2 + 2 * pairs:2].set(taker + moved)
    return tallies[jax.random.permutation(jax.random.fold_in(own_key, 2), count)]


def noise(stream_key, shape, scale, reach, pieces=(), held_as=jnp.bfloat16):
    values = scale * jax.random.normal(stream_key, shape, jnp.float32)
    if pieces:
        values = values * shard_levels(stream_key, shape, pieces, -0.22, 0.18)
    return jnp.clip(values, -reach, reach).astype(held_as)


def setup_inputs(seed: int = 0) -> dict:
    key_list = jax.random.split(jax.random.key(seed), 9)
    query_rows = draw_query_rows(jax.random.fold_in(key_list[8], 71), 0)
    key_rows = draw_key_rows(jax.random.fold_in(key_list[8], 71), 0)
    value_matrix = noise(key_list[2], (WINDOW_TOKENS, KEY_VALUE_HEADS * HEAD_SIZE), 1.0, 6.0, ((0, 32), (1, 8)))
    cotangent = noise(key_list[3], (WINDOW_TOKENS, D), 1.0, 6.0, ((0, 32), (1, 8)))
    frozen_out = noise(key_list[4], (QUERY_HEADS * HEAD_SIZE, D), (QUERY_HEADS * HEAD_SIZE) ** -0.5, 0.078125, ((0, 8),))
    adapter_down = noise(key_list[5], (QUERY_HEADS * HEAD_SIZE, R), (QUERY_HEADS * HEAD_SIZE) ** -0.5, 0.078125, ((0, 8),))
    adapter_up = noise(key_list[6], (R, D), (4 * D) ** -0.5, 0.0390625)
    doc_lengths = uneven_parts(key_list[7], DOCS, WINDOW_TOKENS, WINDOW_TOKENS // 2, 2).astype(jnp.int32)
    return dict(query_rows=query_rows, key_rows=key_rows, value_matrix=value_matrix, cotangent=cotangent, frozen_out=frozen_out, adapter_down=adapter_down, adapter_up=adapter_up, doc_lengths=doc_lengths)


adapter_gain = 2.0
masked_score = -1e30


def document_ids(positions, doc_lengths):
    doc_ends = jnp.cumsum(doc_lengths).astype(jnp.int32)
    return jnp.sum((positions[:, None] >= doc_ends[None, :]).astype(jnp.int32), axis=1)


def reference(query_rows, key_rows, value_matrix, cotangent, frozen_out, adapter_down, adapter_up, doc_lengths):
    score_scale = HEAD_SIZE ** -0.5
    group_width = QUERY_HEADS // KEY_VALUE_HEADS
    rank_grad = jnp.dot(cotangent, adapter_up.T, preferred_element_type=jnp.float32).astype(jnp.bfloat16)
    frozen_part = jnp.dot(cotangent, frozen_out.T, preferred_element_type=jnp.float32)
    adapter_part = jnp.dot(rank_grad, adapter_down.T, preferred_element_type=jnp.float32)
    out_grad = (frozen_part + adapter_gain * adapter_part).astype(jnp.bfloat16)
    positions = jnp.arange(WINDOW_TOKENS, dtype=jnp.int32)
    doc_index = document_ids(positions, doc_lengths)
    allowed = (doc_index[:, None] == doc_index[None, :]) & (positions[:, None] >= positions[None, :])

    def one_head(head):
        kv_index = head // group_width
        head_q = lax.dynamic_slice_in_dim(query_rows, (head * HEAD_SIZE).astype(jnp.int32), HEAD_SIZE, 1)
        head_k = lax.dynamic_slice_in_dim(key_rows, (kv_index * HEAD_SIZE).astype(jnp.int32), HEAD_SIZE, 1)
        head_v = lax.dynamic_slice_in_dim(value_matrix, (kv_index * HEAD_SIZE).astype(jnp.int32), HEAD_SIZE, 1)
        head_dout = lax.dynamic_slice_in_dim(out_grad, (head * HEAD_SIZE).astype(jnp.int32), HEAD_SIZE, 1)
        raw = jnp.dot(head_q, head_k.T, preferred_element_type=jnp.float32) * score_scale
        scores = jnp.where(allowed, raw, masked_score)
        row_top = jnp.max(scores, axis=1, keepdims=True)
        weights = jnp.exp(scores - row_top)
        probs = weights / jnp.sum(weights, axis=1, keepdims=True)
        probs_low = probs.astype(jnp.bfloat16)
        head_out = jnp.dot(probs_low, head_v, preferred_element_type=jnp.float32).astype(jnp.bfloat16)
        delta = jnp.sum(head_dout.astype(jnp.float32) * head_out.astype(jnp.float32), axis=1, keepdims=True)
        dprob = jnp.dot(head_dout, head_v.T, preferred_element_type=jnp.float32)
        dscore = (probs * (dprob - delta)).astype(jnp.bfloat16)
        head_dq = (score_scale * jnp.dot(dscore, head_k, preferred_element_type=jnp.float32)).astype(jnp.bfloat16)
        head_dk = score_scale * jnp.dot(dscore.T, head_q, preferred_element_type=jnp.float32)
        head_dv = jnp.dot(probs_low.T, head_dout, preferred_element_type=jnp.float32)
        return head_out, head_dq, head_dk, head_dv

    head_outs, head_dqs, head_key_grads, head_value_grads = lax.map(one_head, jnp.arange(QUERY_HEADS, dtype=jnp.int32))
    attn_out = jnp.transpose(head_outs, (1, 0, 2)).reshape(WINDOW_TOKENS, QUERY_HEADS * HEAD_SIZE)
    query_grads = jnp.transpose(head_dqs, (1, 0, 2)).reshape(WINDOW_TOKENS, QUERY_HEADS * HEAD_SIZE)
    key_gradient_sum = head_key_grads.reshape(KEY_VALUE_HEADS, group_width, WINDOW_TOKENS, HEAD_SIZE).sum(axis=1)
    value_gradient_sum = head_value_grads.reshape(KEY_VALUE_HEADS, group_width, WINDOW_TOKENS, HEAD_SIZE).sum(axis=1)
    key_gradient = jnp.transpose(key_gradient_sum, (1, 0, 2)).reshape(WINDOW_TOKENS, KEY_VALUE_HEADS * HEAD_SIZE).astype(jnp.bfloat16)
    value_gradient = jnp.transpose(value_gradient_sum, (1, 0, 2)).reshape(WINDOW_TOKENS, KEY_VALUE_HEADS * HEAD_SIZE).astype(jnp.bfloat16)
    rank_acts = jnp.dot(attn_out, adapter_down, preferred_element_type=jnp.float32).astype(jnp.bfloat16)
    down_grad = adapter_gain * jnp.dot(attn_out.T, rank_grad, preferred_element_type=jnp.float32)
    up_grad = adapter_gain * jnp.dot(rank_acts.T, cotangent, preferred_element_type=jnp.float32)
    return query_grads, key_gradient, value_gradient, down_grad, up_grad
```

```python
import math

import jax
import jax.numpy as jnp
from jax import lax
from jax.experimental import pallas as pl
from jax.experimental.pallas import tpu as pltpu
from jax.sharding import PartitionSpec as P

HEAD_SIZE = 128
T = 160
GROUP = 5
N = 896
FEATURES = 640
RANK = 64
SLOTS = 17
SCALE = HEAD_SIZE**-0.5
EXP_SCALE = SCALE * math.log2(math.e)
GAIN = 2.0
MASKED = -1e30
MESH = pl.DeviceIdType.MESH
F32 = jnp.float32
BF16 = jnp.bfloat16

KV = 0
COT = 16
SIB = 25
COL = 33
DEEP = 39
RK = 41
DU_CORE = 48
DU_Y = 49
DU_Z = 52
DU_YBACK = 55
DU_COREBACK = 58
MESSAGES = 59


def dot(left, right, left_dim, right_dim):
    return lax.dot_general(
        left, right, (((left_dim,), (right_dim,)), ((), ())), preferred_element_type=F32
    )


def kernel(
    lengths, q, k, v, cot, w_hbm, up_hbm, down,
    dq_ref, dk_ref, dv_ref, down_ref, up_ref,
    kv, cots, w, qs, scores, probs, dos, acc, parts, sib, col, deep, own,
    rank_in, du, du_core, du_y, du_z, du_sum, send_sem, recv_sem, load_sem,
):
    i = lax.axis_index("ctx")
    mp = lax.axis_index("mp")
    h, y, c = i // 8, (i // 2) % 4, i % 2
    x, zl = mp // 2, mp % 2
    other = 1 - c

    def at(dh=0, dy=0, core=None):
        return (
            ((h + dh + 4) % 4) * 8 + ((y + dy + 4) % 4) * 2 + (c if core is None else core),
            mp,
        )

    def along(dx=0, z=None):
        return (i, ((x + dx + 4) % 4) * 2 + (zl if z is None else z))

    def slot(kind, yy, cc):
        return kind * 8 + cc * 4 + yy

    sent = []

    def send(src, dst, message, device):
        copy = pltpu.make_async_remote_copy(
            src_ref=src, dst_ref=dst, send_sem=send_sem.at[len(sent)], recv_sem=recv_sem.at[message],
            device_id=device, device_id_type=MESH,
        )
        copy.start()
        sent.append(copy)

    def arrived(dst, message):
        pltpu.make_async_remote_copy(
            src_ref=dst, dst_ref=dst, send_sem=send_sem.at[0], recv_sem=recv_sem.at[message],
            device_id=at(core=other), device_id_type=MESH,
        ).wait_recv()

    loads = []
    for b in range(8):
        loads.append(pltpu.make_async_copy(
            w_hbm.at[:, pl.ds(FEATURES * b, FEATURES)], w.at[b, pl.ds(0, FEATURES)], load_sem.at[b]))
        loads.append(pltpu.make_async_copy(
            up_hbm.at[:, pl.ds(FEATURES * b, FEATURES)], w.at[b, pl.ds(FEATURES, RANK)], load_sem.at[8 + b]))
    for load in loads:
        load.start()

    barrier = pltpu.get_barrier_semaphore()
    partners = [at(core=other)]
    partners += [at(dy=d) for d in (1, 2, 3)] + [at(dh=d) for d in (1, 2, 3)]
    partners += [along(dx=d) for d in (1, 2, 3)] + [along(dx=d, z=1 - zl) for d in (0, 1, 2, 3)]
    for partner in partners:
        pl.semaphore_signal(barrier, inc=1, device_id=partner, device_id_type=MESH)
    kv[16, :, 0:HEAD_SIZE] = k[...]
    kv[16, :, HEAD_SIZE:] = v[...]
    cots[mp] = cot[...]
    pl.semaphore_wait(barrier, len(partners))

    g1, mix = slot(0, y, c), slot(1, y, c)
    send(kv.at[16], kv.at[g1], KV + g1, at(dh=1))
    send(kv.at[16], kv.at[mix], KV + mix, at(dh=2))
    send(cots.at[mp], cots.at[mp], COT + 0, along(z=1 - zl))
    send(cots.at[mp], cots.at[mp], COT + 1, along(dx=1))
    send(cots.at[mp], cots.at[mp], COT + 2, along(dx=-1))

    for g in range(GROUP):
        qs[T * g : T * (g + 1), :] = q[:, HEAD_SIZE * g : HEAD_SIZE * (g + 1)]
    qs[T * GROUP : N, :] = jnp.zeros((N - T * GROUP, HEAD_SIZE), BF16)
    token = lax.broadcasted_iota(jnp.int32, (1, N), 1)
    for g in range(GROUP):
        token = token - jnp.where(token >= T, T, 0)
    position = token + i * T
    end0 = lengths[0]
    end1 = end0 + lengths[1]
    end2 = end1 + lengths[2]
    start = jnp.where(
        position >= end2, end2, jnp.where(position >= end1, end1, jnp.where(position >= end0, end0, 0))
    )
    row = lax.broadcasted_iota(jnp.int32, (T, N), 0)

    def score_slots(first, count, bases, top, causal=False):
        keys = kv[pl.ds(first, count), :, 0:HEAD_SIZE].reshape(count * T, HEAD_SIZE)
        raw = dot(keys, qs[...], 1, 1).reshape(count, T, N)
        for s in range(count):
            allowed = row >= start - bases[s]
            if causal:
                allowed = allowed & (row <= token)
            block = jnp.where(allowed, raw[s], MASKED)
            scores[first + s] = block
            top = jnp.maximum(top, jnp.max(block.reshape(T // 8, 8, N), axis=0))
        return top

    def bases_of(kind, cc):
        out = []
        for yy in range(4):
            j = 2 * yy + cc
            if kind == 0:
                group = h - 1
            else:
                group = jnp.where(j < 2 * y + c, h, h - 2)
            out.append((8 * group + j) * T)
        return out

    top = jnp.full((8, N), MASKED, F32)
    top = score_slots(16, 1, [i * T], top, causal=True)

    arrived(kv.at[g1], KV + g1)
    for d in (1, 2, 3):
        send(kv.at[g1], kv.at[g1], KV + g1, at(dy=d))
    send(kv.at[g1], kv.at[g1], KV + g1, at(core=other))

    left, right, far = ((x + 3) % 4) * 2, ((x + 1) % 4) * 2, ((x + 2) % 4) * 2
    half0, half1 = pl.ds(0, T // 2), pl.ds(T // 2, T // 2)
    near = x * 2 + 1 - zl
    arrived(cots.at[left + zl], COT + 1)
    send(cots.at[left + zl, half0], cots.at[left + zl, half0], COT + 5, along(dx=1))
    arrived(cots.at[right + zl], COT + 2)
    send(cots.at[right + zl, half1], cots.at[right + zl, half1], COT + 6, along(dx=-1))
    arrived(cots.at[near], COT + 0)
    send(cots.at[near], cots.at[near], COT + 3, along(dx=1))
    send(cots.at[near], cots.at[near], COT + 4, along(dx=-1))

    arrived(kv.at[mix], KV + mix)
    for d in (1, 2, 3):
        source = jnp.where(y + d < 4, 16, mix)
        send(kv.at[source], kv.at[mix], KV + mix, at(dy=d))
    send(kv.at[jnp.where(c == 0, 16, mix)], kv.at[mix], KV + mix, at(core=other))

    for kind in (0, 1):
        for d in (1, 2, 3):
            s = slot(kind, (y + d) % 4, c)
            arrived(kv.at[s], KV + s)
            send(kv.at[s], kv.at[s], KV + s, at(core=other))
    for load in loads:
        load.wait()

    def project(block):
        acc[...] += dot(cots[block], w[block], 1, 1)

    acc[...] = dot(cots[mp], w[mp], 1, 1)
    project(near)

    for kind in (0, 1):
        top = score_slots(slot(kind, 0, c), 4, bases_of(kind, c), top)

    arrived(cots.at[left + 1 - zl], COT + 3)
    send(cots.at[left + 1 - zl, half0], cots.at[left + 1 - zl, half0], COT + 7, along(dx=1))
    arrived(cots.at[right + 1 - zl], COT + 4)
    send(cots.at[right + 1 - zl, half1], cots.at[right + 1 - zl, half1], COT + 8, along(dx=-1))

    for kind in (0, 1):
        for yy in range(4):
            s = slot(kind, yy, other)
            arrived(kv.at[s], KV + s)
        top = score_slots(slot(kind, 0, other), 4, bases_of(kind, other), top)

    peak = jnp.max(top, axis=0, keepdims=True) * EXP_SCALE
    total = jnp.zeros((8, N), F32)
    out_t = jnp.zeros((HEAD_SIZE, N), F32)
    for first, count in ((0, 4), (4, 4), (8, 4), (12, 4), (16, 1)):
        weights = jnp.exp2(scores[first : first + count].reshape(count * T, N) * EXP_SCALE - peak)
        total = total + jnp.sum(weights.reshape(count * T // 8, 8, N), axis=0)
        low = weights.astype(BF16)
        probs[first : first + count] = low.reshape(count, T, N)
        values = kv[first : first + count, :, HEAD_SIZE:].reshape(count * T, HEAD_SIZE)
        out_t = out_t + dot(values, low, 0, 0)
    inverse = 1.0 / jnp.sum(total, axis=0, keepdims=True)
    out_t = (out_t * inverse).astype(BF16).astype(F32)
    out = out_t.T.astype(BF16)

    rank_part = jnp.zeros((T, RANK), F32)
    for g in range(GROUP):
        rank_part = rank_part + dot(
            out[T * g : T * (g + 1)], down[HEAD_SIZE * g : HEAD_SIZE * (g + 1), :], 1, 0
        )
    rank_in[0] = jnp.concatenate([rank_part[: T // 2], rank_part[T // 2 :]], axis=1).astype(BF16)
    ranks = [along(dx=d) for d in (1, 2, 3)] + [along(dx=d, z=1 - zl) for d in (0, 1, 2, 3)]
    for n, device in enumerate(ranks):
        send(rank_in.at[0], rank_in.at[1 + n], RK + n, device)

    for block in (left + zl, right + zl, left + 1 - zl, right + 1 - zl):
        project(block)
    arrived(cots.at[far + zl, half0], COT + 5)
    arrived(cots.at[far + zl, half1], COT + 6)
    project(far + zl)
    arrived(cots.at[far + 1 - zl, half0], COT + 7)
    arrived(cots.at[far + 1 - zl, half1], COT + 8)
    project(far + 1 - zl)
    rank_grad = acc[:, FEATURES:].astype(BF16)
    out_grad = (acc[:, 0:FEATURES] + GAIN * dot(rank_grad, down[...], 1, 1)).astype(BF16).astype(F32)
    for g in range(GROUP):
        dos[T * g : T * (g + 1), :] = out_grad[:, HEAD_SIZE * g : HEAD_SIZE * (g + 1)]
    dos[T * GROUP : N, :] = jnp.zeros((N - T * GROUP, HEAD_SIZE), F32)
    do_t = dos[...].T * inverse
    delta = jnp.sum(do_t * out_t, axis=0, keepdims=True)
    do_t = do_t.astype(BF16)

    for n in range(7):
        arrived(rank_in.at[1 + n], RK + n)
    rank_sum = rank_in[0].astype(F32)
    for n in range(7):
        rank_sum = rank_sum + rank_in[1 + n].astype(F32)
    rank_acts = jnp.concatenate([rank_sum[:, :RANK], rank_sum[:, RANK:]], axis=0).astype(BF16)
    for g in range(GROUP):
        rows = slice(HEAD_SIZE * g, HEAD_SIZE * (g + 1))
        down_part = GAIN * dot(out[T * g : T * (g + 1)], rank_grad, 0, 0)
        up_part = GAIN * dot(cot[:, rows], rank_acts, 0, 0)
        du[rows, :] = jnp.concatenate([down_part, up_part], axis=1).astype(BF16)
    H = FEATURES // 2
    Q = H // 4
    mine = pl.ds(c * H, H)
    send(du.at[pl.ds(other * H, H)], du_core, DU_CORE, at(core=other))

    def backward(first, count, dq_t):
        keys = kv[pl.ds(first, count), :, 0:HEAD_SIZE].reshape(count * T, HEAD_SIZE)
        values = kv[pl.ds(first, count), :, HEAD_SIZE:].reshape(count * T, HEAD_SIZE)
        low = probs[pl.ds(first, count)].reshape(count * T, N)
        dprob = dot(values, do_t, 1, 0)
        dscore = (low.astype(F32) * (dprob - delta)).astype(BF16)
        dk = dot(dscore, qs[...], 1, 0) * SCALE
        dv = dot(low, do_t, 1, 1)
        if count == 1:
            own[:, 0:HEAD_SIZE] = dk
            own[:, HEAD_SIZE:] = dv
        else:
            parts[pl.ds(first, count), :, 0:HEAD_SIZE] = dk.astype(BF16).reshape(count, T, HEAD_SIZE)
            parts[pl.ds(first, count), :, HEAD_SIZE:] = dv.astype(BF16).reshape(count, T, HEAD_SIZE)
        return dq_t + dot(keys, dscore, 0, 0)

    dq_t = backward(16, 1, jnp.zeros((HEAD_SIZE, N), F32))
    for kind in (1, 0):
        dq_t = backward(slot(kind, 0, other), 4, dq_t)
        for yy in range(4):
            send(parts.at[slot(kind, yy, other)], sib.at[4 * kind + yy], SIB + 4 * kind + yy, at(core=other))
    arrived(du_core, DU_CORE)
    du[mine] = (du[mine].astype(F32) + du_core[...].astype(F32)).astype(BF16)

    def quarter(yy):
        return pl.ds(c * H + yy * Q, Q)

    for d in (1, 2, 3):
        send(du.at[quarter((y + d) % 4)], du_y.at[d - 1], DU_Y + d - 1, at(dy=d))

    for kind in (1, 0):
        dq_t = backward(slot(kind, 0, c), 4, dq_t)
        for yy in range(4):
            arrived(sib.at[4 * kind + yy], SIB + 4 * kind + yy)
        if kind == 0:
            parts[pl.ds(slot(0, 0, c), 4)] = (
                parts[pl.ds(slot(0, 0, c), 4)].astype(F32) + sib[0:4].astype(F32)
            ).astype(BF16)
        else:
            for d in (1, 2, 3):
                s = slot(1, (y + d) % 4, c)
                parts[s] = (parts[s].astype(F32) + sib[4 + (y + d) % 4].astype(F32)).astype(BF16)
            mine_part = sib[4 + y].astype(F32)
            own[...] += mine_part * (1 - c).astype(F32)
            parts[mix] = (parts[mix].astype(F32) + mine_part * c.astype(F32)).astype(BF16)
        for d in (1, 2, 3):
            send(parts.at[slot(kind, (y + d) % 4, c)], col.at[3 * kind + d - 1], COL + 3 * kind + d - 1, at(dy=d))
        if kind == 1:
            total_du = du[quarter(y)].astype(F32)
            for d in (1, 2, 3):
                arrived(du_y.at[d - 1], DU_Y + d - 1)
                total_du = total_du + du_y[d - 1].astype(F32)
            du[quarter(y)] = total_du.astype(BF16)
            for d in (1, 2, 3):
                send(du.at[quarter(y)], du_z.at[d - 1], DU_Z + d - 1, at(dh=d))

    dq = (dq_t * SCALE).T.astype(BF16)
    for g in range(GROUP):
        dq_ref[:, HEAD_SIZE * g : HEAD_SIZE * (g + 1)] = dq[T * g : T * (g + 1), :]

    total_mix = parts[mix].astype(F32)
    for d in (1, 2, 3):
        arrived(col.at[3 + d - 1], COL + 3 + d - 1)
        term = col[3 + d - 1].astype(F32)
        later = jnp.where(y - d < 0, 1.0, 0.0)
        own[...] += term * later
        total_mix = total_mix + term * (1.0 - later)
    parts[mix] = total_mix.astype(BF16)
    send(parts.at[mix], deep.at[1], DEEP + 1, at(dh=-2))

    total_du = du[quarter(y)].astype(F32)
    for d in (1, 2, 3):
        arrived(du_z.at[d - 1], DU_Z + d - 1)
        total_du = total_du + du_z[d - 1].astype(F32)
    du_sum[quarter(y)] = total_du.astype(BF16)
    for d in (1, 2, 3):
        send(du_sum.at[quarter(y)], du_sum.at[quarter(y)], DU_YBACK + d - 1, at(dy=d))

    total_g1 = parts[g1].astype(F32)
    for d in (1, 2, 3):
        arrived(col.at[d - 1], COL + d - 1)
        total_g1 = total_g1 + col[d - 1].astype(F32)
    parts[g1] = total_g1.astype(BF16)
    send(parts.at[g1], deep.at[0], DEEP + 0, at(dh=-1))

    for d in (1, 2, 3):
        arrived(du_sum.at[quarter((y - d + 4) % 4)], DU_YBACK + d - 1)
    send(du_sum.at[mine], du_sum.at[mine], DU_COREBACK, at(core=other))
    arrived(du_sum.at[pl.ds(other * H, H)], DU_COREBACK)
    down_ref[...] = du_sum[:, 0:RANK].astype(F32)
    up_ref[...] = du_sum[:, RANK:].astype(F32).T

    for n in (0, 1):
        arrived(deep.at[n], DEEP + n)
        own[...] += deep[n].astype(F32)
    dk_ref[...] = own[:, 0:HEAD_SIZE].astype(BF16)
    dv_ref[...] = own[:, HEAD_SIZE:].astype(BF16)
    for copy in sent:
        copy.wait_send()


def body(query_rows, key_rows, value_matrix, cotangent, frozen_out, adapter_down, adapter_up, doc_lengths):
    vmem = pl.BlockSpec(memory_space=pltpu.VMEM)
    hbm = pl.BlockSpec(memory_space=pl.ANY)
    return pl.pallas_call(
        kernel,
        out_shape=(
            jax.ShapeDtypeStruct((T, FEATURES), BF16),
            jax.ShapeDtypeStruct((T, HEAD_SIZE), BF16),
            jax.ShapeDtypeStruct((T, HEAD_SIZE), BF16),
            jax.ShapeDtypeStruct((FEATURES, RANK), F32),
            jax.ShapeDtypeStruct((RANK, FEATURES), F32),
        ),
        in_specs=[pl.BlockSpec(memory_space=pltpu.SMEM), vmem, vmem, vmem, vmem, hbm, hbm, vmem],
        out_specs=(vmem,) * 5,
        scratch_shapes=[
            pltpu.VMEM((SLOTS, T, 2 * HEAD_SIZE), BF16),
            pltpu.VMEM((8, T, FEATURES), BF16),
            pltpu.VMEM((8, FEATURES + RANK, FEATURES), BF16),
            pltpu.VMEM((N, HEAD_SIZE), BF16),
            pltpu.VMEM((SLOTS, T, N), F32),
            pltpu.VMEM((SLOTS, T, N), BF16),
            pltpu.VMEM((N, HEAD_SIZE), F32),
            pltpu.VMEM((T, FEATURES + RANK), F32),
            pltpu.VMEM((16, T, 2 * HEAD_SIZE), BF16),
            pltpu.VMEM((8, T, 2 * HEAD_SIZE), BF16),
            pltpu.VMEM((6, T, 2 * HEAD_SIZE), BF16),
            pltpu.VMEM((2, T, 2 * HEAD_SIZE), BF16),
            pltpu.VMEM((T, 2 * HEAD_SIZE), F32),
            pltpu.VMEM((8, T // 2, 2 * RANK), BF16),
            pltpu.VMEM((FEATURES, 2 * RANK), BF16),
            pltpu.VMEM((FEATURES // 2, 2 * RANK), BF16),
            pltpu.VMEM((3, FEATURES // 8, 2 * RANK), BF16),
            pltpu.VMEM((3, FEATURES // 8, 2 * RANK), BF16),
            pltpu.VMEM((FEATURES, 2 * RANK), BF16),
            pltpu.SemaphoreType.DMA((MESSAGES,)),
            pltpu.SemaphoreType.DMA((MESSAGES,)),
            pltpu.SemaphoreType.DMA((16,)),
        ],
        compiler_params=pltpu.CompilerParams(
            collective_id=0, has_side_effects=True, vmem_limit_bytes=60 * 2**20
        ),
    )(
        doc_lengths, query_rows, key_rows, value_matrix, cotangent,
        frozen_out, adapter_up, adapter_down,
    )


def solution(mesh):
    return jax.shard_map(
        body,
        mesh=mesh,
        in_specs=(
            P("ctx", "mp"), P("ctx", "mp"), P("ctx", "mp"), P("ctx", "mp"), P("mp", None), P("mp", None), P(), P(),
        ),
        out_specs=(P("ctx", "mp"), P("ctx", "mp"), P("ctx", "mp"), P("mp", None), P(None, "mp")),
        check_vma=False,
    )
```

```python
import math

import jax
import jax.numpy as jnp
from jax import lax
from jax.experimental import pallas as pl
from jax.experimental.pallas import tpu as pltpu
from jax.sharding import PartitionSpec as P

HEAD_SIZE = 128
T = 160
GROUP = 5
N = 896
FEATURES = 640
RANK = 64
SLOTS = 17
SCALE = HEAD_SIZE**-0.5
EXP_SCALE = SCALE * math.log2(math.e)
GAIN = 2.0
MASKED = -1e30
MESH = pl.DeviceIdType.MESH
F32 = jnp.float32
BF16 = jnp.bfloat16
PIECE = 2 * RANK // 8

KV = 0
COT = 16
SIB = 30
COL = 46
DEEP = 58
RK = 62
DU = 69
DU_Z = 76
DU_BACK = 79
MESSAGES = 86


def dot(left, right, left_dim, right_dim):
    return lax.dot_general(
        left, right, (((left_dim,), (right_dim,)), ((), ())), preferred_element_type=F32
    )


def kernel(
    lengths, q_hbm, k_hbm, v_hbm, cot_hbm, w_hbm, up_hbm, down_hbm,
    dq_out, dk_out, dv_out, down_out, up_out,
    kv, cots, w, down, qs, scores, probs, dos, doc, acc, parts, sib, col, deep, own,
    rank_in, du, du_in, du_z, du_sum, dq_v, dkv_v, du_v, send_sem, recv_sem, load_sem,
):
    i = lax.axis_index("ctx")
    mp = lax.axis_index("mp")
    h, y, c = i // 8, (i // 2) % 4, i % 2
    x, zl = mp // 2, mp % 2
    other = 1 - c

    def at(dh=0, dy=0, core=None):
        return (
            ((h + dh + 4) % 4) * 8 + ((y + dy + 4) % 4) * 2 + (c if core is None else core),
            mp,
        )

    def along(dx=0, z=None):
        return (i, ((x + dx + 4) % 4) * 2 + (zl if z is None else z))

    def slot(kind, yy, cc):
        return kind * 8 + cc * 4 + yy

    sent = []

    def message_to(src, dst, message, device):
        copy = pltpu.make_async_remote_copy(
            src_ref=src, dst_ref=dst, send_sem=send_sem.at[len(sent)], recv_sem=recv_sem.at[message],
            device_id=device, device_id_type=MESH,
        )
        sent.append(copy)
        return copy

    def send(src, dst, message, device):
        message_to(src, dst, message, device).start()

    def arrived(dst, message):
        pltpu.make_async_remote_copy(
            src_ref=dst, dst_ref=dst, send_sem=send_sem.at[0], recv_sem=recv_sem.at[message],
            device_id=at(core=other), device_id_type=MESH,
        ).wait_recv()

    barrier = pltpu.get_barrier_semaphore()
    plane = [(d, cc) for d in (0, 1, 2, 3) for cc in (0, 1) if (d, cc) != (0, 0)]
    ranks = [along(dx=d) for d in (1, 2, 3)] + [along(dx=d, z=1 - zl) for d in (0, 1, 2, 3)]
    partners = [at(dy=d, core=(c + cc) % 2) for d, cc in plane] + [at(dh=d) for d in (1, 2, 3)] + ranks
    for partner in partners:
        pl.semaphore_signal(barrier, inc=1, device_id=partner, device_id_type=MESH)

    loads = []

    def load(src, dst):
        loads.append(pltpu.make_async_copy(src, dst, load_sem.at[len(loads)]))
        loads[-1].start()

    load(k_hbm, kv.at[16, :, pl.ds(0, HEAD_SIZE)])
    load(v_hbm, kv.at[16, :, pl.ds(HEAD_SIZE, HEAD_SIZE)])
    load(cot_hbm, cots.at[mp])
    for g in range(GROUP):
        load(q_hbm.at[:, pl.ds(HEAD_SIZE * g, HEAD_SIZE)], qs.at[pl.ds(T * g, T)])
    load(down_hbm, down)
    for b in range(8):
        load(w_hbm.at[:, pl.ds(FEATURES * b, FEATURES)], w.at[b, pl.ds(0, FEATURES)])
        load(up_hbm.at[:, pl.ds(FEATURES * b, FEATURES)], w.at[b, pl.ds(FEATURES, RANK)])
    qs[T * GROUP : N, :] = jnp.zeros((N - T * GROUP, HEAD_SIZE), BF16)
    for copy in loads[0:3]:
        copy.wait()
    pl.semaphore_wait(barrier, len(partners))

    g1, mix = slot(0, y, c), slot(1, y, c)
    near = x * 2 + 1 - zl
    left, right, far = ((x + 3) % 4) * 2, ((x + 1) % 4) * 2, ((x + 2) % 4) * 2
    half0, half1 = pl.ds(0, T // 2), pl.ds(T // 2, T // 2)
    halves = (half0, half1)

    def half(block, n):
        return cots.at[block, halves[n]]

    for n in (0, 1):
        send(half(mp, n), half(mp, n), COT + 2 + n, along(dx=1))
        send(half(mp, 1 - n), half(mp, 1 - n), COT + 5 - n, along(dx=-1))
    send(kv.at[16], kv.at[g1], KV + g1, at(dh=1))
    send(kv.at[16], kv.at[mix], KV + mix, at(dh=2))
    send(half(mp, 0), half(mp, 0), COT + 0, along(z=1 - zl))
    send(half(mp, 1), half(mp, 1), COT + 1, along(z=1 - zl))
    early, late = [], []
    for d in (1, 2, 3):
        copy = message_to(kv.at[16], kv.at[mix], KV + mix, at(dy=d))
        early.append((y + d < 4, copy))
        late.append((y + d >= 4, pltpu.make_async_remote_copy(
            src_ref=kv.at[mix], dst_ref=kv.at[mix], send_sem=send_sem.at[len(sent) - 1],
            recv_sem=recv_sem.at[KV + mix], device_id=at(dy=d), device_id_type=MESH)))
    copy = message_to(kv.at[16], kv.at[mix], KV + mix, at(core=other))
    early.append((c == 0, copy))
    late.append((c == 1, pltpu.make_async_remote_copy(
        src_ref=kv.at[mix], dst_ref=kv.at[mix], send_sem=send_sem.at[len(sent) - 1],
        recv_sem=recv_sem.at[KV + mix], device_id=at(core=other), device_id_type=MESH)))
    for condition, copy in early:
        pl.when(condition)(copy.start)

    token = lax.broadcasted_iota(jnp.int32, (1, N), 1)
    for g in range(GROUP):
        token = token - jnp.where(token >= T, T, 0)
    position = token + i * T
    end0 = lengths[0]
    end1 = end0 + lengths[1]
    end2 = end1 + lengths[2]
    start = jnp.where(
        position >= end2, end2, jnp.where(position >= end1, end1, jnp.where(position >= end0, end0, 0))
    )
    row = lax.broadcasted_iota(jnp.int32, (T, N), 0)

    def forward(first, count, bases, state, causal=False):
        keys = kv[pl.ds(first, count), :, 0:HEAD_SIZE].reshape(count * T, HEAD_SIZE)
        values = kv[pl.ds(first, count), :, HEAD_SIZE:].reshape(count * T, HEAD_SIZE)
        raw = dot(keys, qs[...], 1, 1).reshape(count, T, N)
        top = jnp.full((8, N), MASKED, F32)
        for s in range(count):
            allowed = row >= start - bases[s]
            if causal:
                allowed = allowed & (row <= token)
            block = jnp.where(allowed, raw[s], MASKED)
            scores[s] = block
            top = jnp.maximum(top, jnp.max(block.reshape(T // 8, 8, N), axis=0))
        peak = jnp.max(top, axis=0, keepdims=True) * EXP_SCALE
        if state is not None:
            peak = jnp.maximum(peak, state[0])
        weights = jnp.exp2(scores[0:count].reshape(count * T, N) * EXP_SCALE - peak)
        total = jnp.sum(weights.reshape(count * T // 8, 8, N), axis=0)
        low = weights.astype(BF16)
        probs[pl.ds(first, count)] = low.reshape(count, T, N)
        out_t = dot(values, low, 0, 0)
        if state is not None:
            decay = jnp.exp2(state[0] - peak)
            total = total + state[1] * decay
            out_t = out_t + state[2] * decay
        return peak, total, out_t

    def bases_of(kind, cc):
        out = []
        for yy in range(4):
            j = 2 * yy + cc
            if kind == 0:
                group = h - 1
            else:
                group = jnp.where(j < 2 * y + c, h, h - 2)
            out.append((8 * group + j) * T)
        return out

    def project(block):
        acc[...] += dot(cots[block], w[block], 1, 1)

    for copy in loads[3:8]:
        copy.wait()
    peaks = {}
    state = forward(16, 1, [i * T], None, causal=True)
    peaks["own"] = state[0]

    arrived(half(left + zl, 0), COT + 2)
    send(half(left + zl, 0), half(left + zl, 0), COT + 6, along(dx=1))
    arrived(half(right + zl, 1), COT + 5)
    send(half(right + zl, 1), half(right + zl, 1), COT + 7, along(dx=-1))
    arrived(kv.at[g1], KV + g1)
    for d in (1, 2, 3):
        send(kv.at[g1], kv.at[g1], KV + g1, at(dy=d))
    send(kv.at[g1], kv.at[g1], KV + g1, at(core=other))
    arrived(kv.at[mix], KV + mix)
    for condition, copy in late:
        pl.when(condition)(copy.start)
    arrived(half(near, 0), COT + 0)
    send(half(near, 0), half(near, 0), COT + 8, along(dx=1))
    arrived(half(near, 1), COT + 1)
    send(half(near, 1), half(near, 1), COT + 11, along(dx=-1))
    send(half(near, 1), half(near, 1), COT + 9, along(dx=1))
    send(half(near, 0), half(near, 0), COT + 10, along(dx=-1))
    for copy in loads[8:]:
        copy.wait()
    acc[...] = dot(cots[mp], w[mp], 1, 1)
    project(near)

    for kind in (0, 1):
        for d in (1, 2, 3):
            s = slot(kind, (y + d) % 4, c)
            arrived(kv.at[s], KV + s)
            send(kv.at[s], kv.at[s], KV + s, at(core=other))
        state = forward(slot(kind, 0, c), 4, bases_of(kind, c), state)
        peaks[kind, 0] = state[0]
        if kind == 0:
            arrived(half(left + 1 - zl, 0), COT + 8)
            send(half(left + 1 - zl, 0), half(left + 1 - zl, 0), COT + 12, along(dx=1))
            arrived(half(right + 1 - zl, 1), COT + 11)
            send(half(right + 1 - zl, 1), half(right + 1 - zl, 1), COT + 13, along(dx=-1))

    arrived(half(left + zl, 1), COT + 3)
    arrived(half(right + zl, 0), COT + 4)
    for block in (left + zl, right + zl):
        project(block)
    for kind in (0, 1):
        for yy in range(4):
            s = slot(kind, yy, other)
            arrived(kv.at[s], KV + s)
        state = forward(slot(kind, 0, other), 4, bases_of(kind, other), state)
        peaks[kind, 1] = state[0]

    peak, total, out_t = state
    inverse = 1.0 / jnp.sum(total, axis=0, keepdims=True)
    out_t = (out_t * inverse).astype(BF16).astype(F32)
    out = out_t.T.astype(BF16)

    rank_part = jnp.zeros((T, RANK), F32)
    for g in range(GROUP):
        rank_part = rank_part + dot(
            out[T * g : T * (g + 1)], down[:, HEAD_SIZE * g : HEAD_SIZE * (g + 1)], 1, 1
        )
    rank_in[0] = jnp.concatenate([rank_part[: T // 2], rank_part[T // 2 :]], axis=1).astype(BF16)
    for n, device in enumerate(ranks):
        send(rank_in.at[0], rank_in.at[1 + n], RK + n, device)

    arrived(half(left + 1 - zl, 1), COT + 9)
    project(left + 1 - zl)
    arrived(half(right + 1 - zl, 0), COT + 10)
    project(right + 1 - zl)
    arrived(half(far + zl, 0), COT + 6)
    arrived(half(far + zl, 1), COT + 7)
    project(far + zl)
    arrived(half(far + 1 - zl, 0), COT + 12)
    arrived(half(far + 1 - zl, 1), COT + 13)
    project(far + 1 - zl)
    rank_grad = acc[:, FEATURES:].astype(BF16)
    out_grad = (acc[:, 0:FEATURES] + GAIN * dot(rank_grad, down[...], 1, 0)).astype(BF16).astype(F32)
    for g in range(GROUP):
        dos[T * g : T * (g + 1), :] = out_grad[:, HEAD_SIZE * g : HEAD_SIZE * (g + 1)]
    dos[T * GROUP : N, :] = jnp.zeros((N - T * GROUP, HEAD_SIZE), F32)
    do_t = dos[...].T * inverse
    delta = jnp.sum(do_t * out_t, axis=0, keepdims=True)

    chunks = [("own", 16, 1)]
    chunks += [((kind, k), slot(kind, 0, c if k == 0 else other), 4) for k in (1, 0) for kind in (1, 0)]
    deltas, place = {}, {}
    for n, (key, first, count) in enumerate(chunks):
        factor = jnp.exp2(peaks[key] - peak)
        doc[n] = (do_t * factor).astype(BF16)
        deltas[key] = delta * factor
        place[key] = n

    def value_part(key, first, count):
        low = probs[pl.ds(first, count)].reshape(count * T, N)
        dv = dot(low, doc[place[key]], 1, 1)
        if count == 1:
            own[1] = dv
        else:
            parts[1, pl.ds(first, count)] = dv.astype(BF16).reshape(count, T, HEAD_SIZE)

    def key_part(key, first, count, dq_t):
        keys = kv[pl.ds(first, count), :, 0:HEAD_SIZE].reshape(count * T, HEAD_SIZE)
        values = kv[pl.ds(first, count), :, HEAD_SIZE:].reshape(count * T, HEAD_SIZE)
        low = probs[pl.ds(first, count)].reshape(count * T, N)
        dprob = dot(values, doc[place[key]], 1, 0)
        dscore = (low.astype(F32) * (dprob - deltas[key])).astype(BF16)
        dk = dot(dscore, qs[...], 1, 0) * SCALE
        if count == 1:
            own[0] = dk
        else:
            parts[0, pl.ds(first, count)] = dk.astype(BF16).reshape(count, T, HEAD_SIZE)
        return dq_t + dot(keys, dscore, 0, 0)

    def to_other_core(kv_of, kind):
        for yy in range(4):
            n = 4 * kind + yy
            send(parts.at[kv_of, slot(kind, yy, other)], sib.at[kv_of, n], SIB + 8 * kv_of + n, at(core=other))

    def along_y(kv_of, kind):
        for yy in range(4):
            n = 4 * kind + yy
            arrived(sib.at[kv_of, n], SIB + 8 * kv_of + n)
        for d in (1, 2, 3):
            yy = (y + d) % 4
            s = slot(kind, yy, c)
            parts[kv_of, s] = (parts[kv_of, s].astype(F32) + sib[kv_of, 4 * kind + yy].astype(F32)).astype(BF16)
            n = 6 * kv_of + 3 * kind + d - 1
            send(parts.at[kv_of, s], col.at[n], COL + n, at(dy=d))
        term = sib[kv_of, 4 * kind + y].astype(F32)
        if kind == 0:
            parts[kv_of, g1] = (parts[kv_of, g1].astype(F32) + term).astype(BF16)
        else:
            own[kv_of] += term * (1 - c).astype(F32)
            parts[kv_of, mix] = (parts[kv_of, mix].astype(F32) + term * c.astype(F32)).astype(BF16)

    def along_z(kv_of, kind):
        s = mix if kind == 1 else g1
        total = parts[kv_of, s].astype(F32)
        for d in (1, 2, 3):
            n = 6 * kv_of + 3 * kind + d - 1
            arrived(col.at[n], COL + n)
            term = col[n].astype(F32)
            if kind == 1:
                later = jnp.where(y - d < 0, 1.0, 0.0)
                own[kv_of] += term * later
                term = term * (1.0 - later)
            total = total + term
        parts[kv_of, s] = total.astype(BF16)
        n = 2 * kv_of + kind
        send(parts.at[kv_of, s], deep.at[n], DEEP + n, at(dh=-1 - kind))

    by_key = {key: (key, first, count) for key, first, count in chunks}
    for kind in (1, 0):
        value_part(*by_key[kind, 1])
        to_other_core(1, kind)
    value_part(*by_key["own"])
    for kind in (1, 0):
        value_part(*by_key[kind, 0])

    for n in range(7):
        arrived(rank_in.at[1 + n], RK + n)
    rank_sum = rank_in[0].astype(F32)
    for n in range(7):
        rank_sum = rank_sum + rank_in[1 + n].astype(F32)
    rank_acts = jnp.concatenate([rank_sum[:, :RANK], rank_sum[:, RANK:]], axis=0).astype(BF16)
    for g in range(GROUP):
        du[0:RANK, HEAD_SIZE * g : HEAD_SIZE * (g + 1)] = (
            GAIN * dot(rank_grad, out[T * g : T * (g + 1)], 0, 0)
        ).astype(BF16)
    du[RANK:, :] = (GAIN * dot(rank_acts, cots[mp], 0, 0)).astype(BF16)

    def piece(yy, cc):
        return pl.ds((yy * 2 + cc) * PIECE, PIECE)

    for n, (d, cc) in enumerate(plane):
        yy, core = (y + d) % 4, (c + cc) % 2
        send(du.at[piece(yy, core)], du_in.at[n], DU + n, at(dy=d, core=core))

    for kind in (1, 0):
        along_y(1, kind)
    dq_t = key_part(*by_key["own"], jnp.zeros((HEAD_SIZE, N), F32))
    for kind in (1, 0):
        dq_t = key_part(*by_key[kind, 1], dq_t)
        to_other_core(0, kind)

    total_du = du[piece(y, c)].astype(F32)
    for n in range(7):
        arrived(du_in.at[n], DU + n)
        total_du = total_du + du_in[n].astype(F32)
    du_z[3] = total_du.astype(BF16)
    for d in (1, 2, 3):
        send(du_z.at[3], du_z.at[d - 1], DU_Z + d - 1, at(dh=d))

    for kind in (1, 0):
        dq_t = key_part(*by_key[kind, 0], dq_t)
        along_y(0, kind)
    for kind in (1, 0):
        along_z(1, kind)

    for d in (1, 2, 3):
        arrived(du_z.at[d - 1], DU_Z + d - 1)
        total_du = total_du + du_z[d - 1].astype(F32)
    du_sum[piece(y, c)] = total_du.astype(BF16)
    for n, (d, cc) in enumerate(plane):
        send(du_sum.at[piece(y, c)], du_sum.at[piece(y, c)], DU_BACK + n, at(dy=d, core=(c + cc) % 2))

    results = []

    def store(src, dst):
        results.append(pltpu.make_async_copy(src, dst, load_sem.at[len(loads) + len(results)]))
        results[-1].start()

    dq = (dq_t * SCALE).T.astype(BF16)
    for g in range(GROUP):
        dq_v[:, HEAD_SIZE * g : HEAD_SIZE * (g + 1)] = dq[T * g : T * (g + 1), :]
    store(dq_v, dq_out)

    for kind in (1, 0):
        along_z(0, kind)

    for n, (d, cc) in enumerate(plane):
        arrived(du_sum.at[piece((y - d + 4) % 4, (c + cc) % 2)], DU_BACK + n)
    du_v[...] = du_sum[...].astype(F32)
    store(du_v.at[pl.ds(0, RANK)], down_out)
    store(du_v.at[pl.ds(RANK, RANK)], up_out)

    for kv_of, result in ((1, dv_out), (0, dk_out)):
        total = own[kv_of]
        for kind in (1, 0):
            arrived(deep.at[2 * kv_of + kind], DEEP + 2 * kv_of + kind)
            total = total + deep[2 * kv_of + kind].astype(F32)
        dkv_v[kv_of] = total.astype(BF16)
        store(dkv_v.at[kv_of], result)
    for copy in sent:
        copy.wait_send()
    for copy in results:
        copy.wait()


def hand_on(*refs):
    for n in range(5):
        refs[5 + n][...] = refs[n][...]


def body(query_rows, key_rows, value_matrix, cotangent, frozen_out, adapter_down, adapter_up, doc_lengths):
    hbm = pl.BlockSpec(memory_space=pl.ANY)
    shapes = (
        jax.ShapeDtypeStruct((T, FEATURES), BF16),
        jax.ShapeDtypeStruct((T, HEAD_SIZE), BF16),
        jax.ShapeDtypeStruct((T, HEAD_SIZE), BF16),
        jax.ShapeDtypeStruct((RANK, FEATURES), F32),
        jax.ShapeDtypeStruct((RANK, FEATURES), F32),
    )
    outs = pl.pallas_call(
        kernel,
        out_shape=shapes,
        in_specs=[pl.BlockSpec(memory_space=pltpu.SMEM)] + [hbm] * 7,
        out_specs=(hbm,) * 5,
        scratch_shapes=[
            pltpu.VMEM((SLOTS, T, 2 * HEAD_SIZE), BF16),
            pltpu.VMEM((8, T, FEATURES), BF16),
            pltpu.VMEM((8, FEATURES + RANK, FEATURES), BF16),
            pltpu.VMEM((RANK, FEATURES), BF16),
            pltpu.VMEM((N, HEAD_SIZE), BF16),
            pltpu.VMEM((4, T, N), F32),
            pltpu.VMEM((SLOTS, T, N), BF16),
            pltpu.VMEM((N, HEAD_SIZE), F32),
            pltpu.VMEM((5, HEAD_SIZE, N), BF16),
            pltpu.VMEM((T, FEATURES + RANK), F32),
            pltpu.VMEM((2, 16, T, HEAD_SIZE), BF16),
            pltpu.VMEM((2, 8, T, HEAD_SIZE), BF16),
            pltpu.VMEM((12, T, HEAD_SIZE), BF16),
            pltpu.VMEM((4, T, HEAD_SIZE), BF16),
            pltpu.VMEM((2, T, HEAD_SIZE), F32),
            pltpu.VMEM((8, T // 2, 2 * RANK), BF16),
            pltpu.VMEM((2 * RANK, FEATURES), BF16),
            pltpu.VMEM((7, PIECE, FEATURES), BF16),
            pltpu.VMEM((4, PIECE, FEATURES), BF16),
            pltpu.VMEM((2 * RANK, FEATURES), BF16),
            pltpu.VMEM((T, FEATURES), BF16),
            pltpu.VMEM((2, T, HEAD_SIZE), BF16),
            pltpu.VMEM((2 * RANK, FEATURES), F32),
            pltpu.SemaphoreType.DMA((MESSAGES,)),
            pltpu.SemaphoreType.DMA((MESSAGES,)),
            pltpu.SemaphoreType.DMA((32,)),
        ],
        compiler_params=pltpu.CompilerParams(
            collective_id=0, has_side_effects=True, vmem_limit_bytes=60 * 2**20
        ),
    )(
        doc_lengths, query_rows, key_rows, value_matrix, cotangent,
        frozen_out, adapter_up, adapter_down.T,
    )
    dq, dk, dv, down_t, up = pl.pallas_call(
        hand_on,
        out_shape=shapes,
        in_specs=[pl.BlockSpec(memory_space=pltpu.VMEM)] * 5,
        out_specs=(pl.BlockSpec(memory_space=pltpu.VMEM),) * 5,
    )(*outs)
    return dq, dk, dv, down_t.T, up


def solution(mesh):
    return jax.shard_map(
        body,
        mesh=mesh,
        in_specs=(
            P("ctx", "mp"), P("ctx", "mp"), P("ctx", "mp"), P("ctx", "mp"), P("mp", None), P("mp", None), P(), P(),
        ),
        out_specs=(P("ctx", "mp"), P("ctx", "mp"), P("ctx", "mp"), P("mp", None), P(None, "mp")),
        check_vma=False,
    )
```

```python
import math

import jax
import jax.numpy as jnp
from jax import lax
from jax.experimental import pallas as pl
from jax.experimental.pallas import tpu as pltpu
from jax.sharding import PartitionSpec as P

HEAD_SIZE = 128
T = 160
GROUP = 5
N = 896
FEATURES = 640
RANK = 64
SLOTS = 17
SCALE = HEAD_SIZE**-0.5
EXP_SCALE = SCALE * math.log2(math.e)
GAIN = 2.0
MASKED = -1e30
MESH = pl.DeviceIdType.MESH
F32 = jnp.float32
BF16 = jnp.bfloat16
PIECE = 2 * RANK // 8

KV = 0
COT = 16
SIB = 30
COL = 46
DEEP = 58
RK = 62
DU = 69
DU_Z = 76
DU_BACK = 79
MESSAGES = 86


def dot(left, right, left_dim, right_dim):
    return lax.dot_general(
        left, right, (((left_dim,), (right_dim,)), ((), ())), preferred_element_type=F32
    )


def kernel(
    lengths, q_hbm, k_hbm, v_hbm, cot_hbm, w_hbm, up_hbm, down_hbm,
    dq_out, dk_out, dv_out, down_out, up_out,
    kv, cots, w, down, qs, scores, probs, dos, doc, acc, parts, sib, col, deep, own,
    rank_in, du, du_in, du_z, du_sum, dq_v, dkv_v, du_v, send_sem, recv_sem, load_sem,
):
    i = lax.axis_index("ctx")
    mp = lax.axis_index("mp")
    h, y, c = i // 8, (i // 2) % 4, i % 2
    x, zl = mp // 2, mp % 2
    other = 1 - c

    def at(dh=0, dy=0, core=None):
        return (
            ((h + dh + 4) % 4) * 8 + ((y + dy + 4) % 4) * 2 + (c if core is None else core),
            mp,
        )

    def along(dx=0, z=None):
        return (i, ((x + dx + 4) % 4) * 2 + (zl if z is None else z))

    def slot(kind, yy, cc):
        return kind * 8 + cc * 4 + yy

    sent = []

    def message_to(src, dst, message, device):
        copy = pltpu.make_async_remote_copy(
            src_ref=src, dst_ref=dst, send_sem=send_sem.at[len(sent)], recv_sem=recv_sem.at[message],
            device_id=device, device_id_type=MESH,
        )
        sent.append(copy)
        return copy

    def send(src, dst, message, device):
        message_to(src, dst, message, device).start()

    def arrived(dst, message):
        pltpu.make_async_remote_copy(
            src_ref=dst, dst_ref=dst, send_sem=send_sem.at[0], recv_sem=recv_sem.at[message],
            device_id=at(core=other), device_id_type=MESH,
        ).wait_recv()

    barrier = pltpu.get_barrier_semaphore()
    plane = [(d, cc) for d in (0, 1, 2, 3) for cc in (0, 1) if (d, cc) != (0, 0)]
    ranks = [along(dx=d) for d in (1, 2, 3)] + [along(dx=d, z=1 - zl) for d in (0, 1, 2, 3)]
    partners = [at(dh=d) for d in (2, 1, 3)] + ranks + [at(dy=d, core=(c + cc) % 2) for d, cc in plane]
    for partner in partners:
        pl.semaphore_signal(barrier, inc=1, device_id=partner, device_id_type=MESH)

    loads = []

    def load(src, dst):
        loads.append(pltpu.make_async_copy(src, dst, load_sem.at[len(loads)]))
        loads[-1].start()

    load(k_hbm, kv.at[16, :, pl.ds(0, HEAD_SIZE)])
    load(v_hbm, kv.at[16, :, pl.ds(HEAD_SIZE, HEAD_SIZE)])
    load(cot_hbm, cots.at[mp])
    qs[T * GROUP : N, :] = jnp.zeros((N - T * GROUP, HEAD_SIZE), BF16)
    for copy in loads[0:3]:
        copy.wait()
    pl.semaphore_wait(barrier, len(partners))

    g1, mix = slot(0, y, c), slot(1, y, c)
    near = x * 2 + 1 - zl
    left, right, far = ((x + 3) % 4) * 2, ((x + 1) % 4) * 2, ((x + 2) % 4) * 2
    half0, half1 = pl.ds(0, T // 2), pl.ds(T // 2, T // 2)
    halves = (half0, half1)

    def half(block, n):
        return cots.at[block, halves[n]]

    send(kv.at[16], kv.at[g1], KV + g1, at(dh=1))
    send(kv.at[16], kv.at[mix], KV + mix, at(dh=2))
    for n in (0, 1):
        send(half(mp, n), half(mp, n), COT + 2 + n, along(dx=1))
        send(half(mp, 1 - n), half(mp, 1 - n), COT + 5 - n, along(dx=-1))
    send(half(mp, 0), half(mp, 0), COT + 0, along(z=1 - zl))
    send(half(mp, 1), half(mp, 1), COT + 1, along(z=1 - zl))
    early, late = [], []
    for d in (1, 2, 3):
        copy = message_to(kv.at[16], kv.at[mix], KV + mix, at(dy=d))
        early.append((y + d < 4, copy))
        late.append((y + d >= 4, pltpu.make_async_remote_copy(
            src_ref=kv.at[mix], dst_ref=kv.at[mix], send_sem=send_sem.at[len(sent) - 1],
            recv_sem=recv_sem.at[KV + mix], device_id=at(dy=d), device_id_type=MESH)))
    copy = message_to(kv.at[16], kv.at[mix], KV + mix, at(core=other))
    early.append((c == 0, copy))
    late.append((c == 1, pltpu.make_async_remote_copy(
        src_ref=kv.at[mix], dst_ref=kv.at[mix], send_sem=send_sem.at[len(sent) - 1],
        recv_sem=recv_sem.at[KV + mix], device_id=at(core=other), device_id_type=MESH)))
    for condition, copy in early:
        pl.when(condition)(copy.start)

    for g in range(GROUP):
        load(q_hbm.at[:, pl.ds(HEAD_SIZE * g, HEAD_SIZE)], qs.at[pl.ds(T * g, T)])
    load(down_hbm, down)
    for b in range(8):
        load(w_hbm.at[:, pl.ds(FEATURES * b, FEATURES)], w.at[b, pl.ds(0, FEATURES)])
        load(up_hbm.at[:, pl.ds(FEATURES * b, FEATURES)], w.at[b, pl.ds(FEATURES, RANK)])

    token = lax.broadcasted_iota(jnp.int32, (1, N), 1)
    for g in range(GROUP):
        token = token - jnp.where(token >= T, T, 0)
    position = token + i * T
    end0 = lengths[0]
    end1 = end0 + lengths[1]
    end2 = end1 + lengths[2]
    start = jnp.where(
        position >= end2, end2, jnp.where(position >= end1, end1, jnp.where(position >= end0, end0, 0))
    )
    row = lax.broadcasted_iota(jnp.int32, (T, N), 0)

    def forward(first, count, bases, state, causal=False):
        keys = kv[pl.ds(first, count), :, 0:HEAD_SIZE].reshape(count * T, HEAD_SIZE)
        values = kv[pl.ds(first, count), :, HEAD_SIZE:].reshape(count * T, HEAD_SIZE)
        raw = dot(keys, qs[...], 1, 1).reshape(count, T, N)
        top = jnp.full((8, N), MASKED, F32)
        for s in range(count):
            allowed = row >= start - bases[s]
            if causal:
                allowed = allowed & (row <= token)
            block = jnp.where(allowed, raw[s], MASKED)
            scores[s] = block
            top = jnp.maximum(top, jnp.max(block.reshape(T // 8, 8, N), axis=0))
        peak = jnp.max(top, axis=0, keepdims=True) * EXP_SCALE
        if state is not None:
            peak = jnp.maximum(peak, state[0])
        weights = jnp.exp2(scores[0:count].reshape(count * T, N) * EXP_SCALE - peak)
        total = jnp.sum(weights.reshape(count * T // 8, 8, N), axis=0)
        low = weights.astype(BF16)
        probs[pl.ds(first, count)] = low.reshape(count, T, N)
        out_t = dot(values, low, 0, 0)
        if state is not None:
            decay = jnp.exp2(state[0] - peak)
            total = total + state[1] * decay
            out_t = out_t + state[2] * decay
        return peak, total, out_t

    def bases_of(kind, cc):
        out = []
        for yy in range(4):
            j = 2 * yy + cc
            if kind == 0:
                group = h - 1
            else:
                group = jnp.where(j < 2 * y + c, h, h - 2)
            out.append((8 * group + j) * T)
        return out

    def project(block):
        acc[...] += dot(cots[block], w[block], 1, 1)

    for copy in loads[3:8]:
        copy.wait()
    peaks = {}
    state = forward(16, 1, [i * T], None, causal=True)
    peaks["own"] = state[0]

    arrived(half(left + zl, 0), COT + 2)
    send(half(left + zl, 0), half(left + zl, 0), COT + 6, along(dx=1))
    arrived(half(right + zl, 1), COT + 5)
    send(half(right + zl, 1), half(right + zl, 1), COT + 7, along(dx=-1))
    arrived(kv.at[g1], KV + g1)
    for d in (1, 2, 3):
        send(kv.at[g1], kv.at[g1], KV + g1, at(dy=d))
    send(kv.at[g1], kv.at[g1], KV + g1, at(core=other))
    arrived(kv.at[mix], KV + mix)
    for condition, copy in late:
        pl.when(condition)(copy.start)
    arrived(half(near, 0), COT + 0)
    send(half(near, 0), half(near, 0), COT + 8, along(dx=1))
    arrived(half(near, 1), COT + 1)
    send(half(near, 1), half(near, 1), COT + 11, along(dx=-1))
    send(half(near, 1), half(near, 1), COT + 9, along(dx=1))
    send(half(near, 0), half(near, 0), COT + 10, along(dx=-1))
    for copy in loads[8:]:
        copy.wait()
    acc[...] = dot(cots[mp], w[mp], 1, 1)
    project(near)

    for kind in (0, 1):
        for d in (1, 2, 3):
            s = slot(kind, (y + d) % 4, c)
            arrived(kv.at[s], KV + s)
            send(kv.at[s], kv.at[s], KV + s, at(core=other))
        state = forward(slot(kind, 0, c), 4, bases_of(kind, c), state)
        peaks[kind, 0] = state[0]
        if kind == 0:
            arrived(half(left + 1 - zl, 0), COT + 8)
            send(half(left + 1 - zl, 0), half(left + 1 - zl, 0), COT + 12, along(dx=1))
            arrived(half(right + 1 - zl, 1), COT + 11)
            send(half(right + 1 - zl, 1), half(right + 1 - zl, 1), COT + 13, along(dx=-1))

    arrived(half(left + zl, 1), COT + 3)
    arrived(half(right + zl, 0), COT + 4)
    for block in (left + zl, right + zl):
        project(block)
    for kind in (0, 1):
        for yy in range(4):
            s = slot(kind, yy, other)
            arrived(kv.at[s], KV + s)
        state = forward(slot(kind, 0, other), 4, bases_of(kind, other), state)
        peaks[kind, 1] = state[0]

    peak, total, out_t = state
    inverse = 1.0 / jnp.sum(total, axis=0, keepdims=True)
    out_t = (out_t * inverse).astype(BF16).astype(F32)
    out = out_t.T.astype(BF16)

    rank_part = jnp.zeros((T, RANK), F32)
    for g in range(GROUP):
        rank_part = rank_part + dot(
            out[T * g : T * (g + 1)], down[:, HEAD_SIZE * g : HEAD_SIZE * (g + 1)], 1, 1
        )
    rank_in[0] = jnp.concatenate([rank_part[: T // 2], rank_part[T // 2 :]], axis=1).astype(BF16)
    for n, device in enumerate(ranks):
        send(rank_in.at[0], rank_in.at[1 + n], RK + n, device)

    arrived(half(left + 1 - zl, 1), COT + 9)
    project(left + 1 - zl)
    arrived(half(right + 1 - zl, 0), COT + 10)
    project(right + 1 - zl)
    arrived(half(far + zl, 0), COT + 6)
    arrived(half(far + zl, 1), COT + 7)
    project(far + zl)
    arrived(half(far + 1 - zl, 0), COT + 12)
    arrived(half(far + 1 - zl, 1), COT + 13)
    project(far + 1 - zl)
    rank_grad = acc[:, FEATURES:].astype(BF16)
    out_grad = (acc[:, 0:FEATURES] + GAIN * dot(rank_grad, down[...], 1, 0)).astype(BF16).astype(F32)
    for g in range(GROUP):
        dos[T * g : T * (g + 1), :] = out_grad[:, HEAD_SIZE * g : HEAD_SIZE * (g + 1)]
    dos[T * GROUP : N, :] = jnp.zeros((N - T * GROUP, HEAD_SIZE), F32)
    do_t = dos[...].T * inverse
    delta = jnp.sum(do_t * out_t, axis=0, keepdims=True)

    chunks = [("own", 16, 1)]
    chunks += [((kind, k), slot(kind, 0, c if k == 0 else other), 4) for k in (1, 0) for kind in (1, 0)]
    deltas, place = {}, {}
    for n, (key, first, count) in enumerate(chunks):
        factor = jnp.exp2(peaks[key] - peak)
        doc[n] = (do_t * factor).astype(BF16)
        deltas[key] = delta * factor
        place[key] = n

    def value_part(key, first, count):
        low = probs[pl.ds(first, count)].reshape(count * T, N)
        dv = dot(low, doc[place[key]], 1, 1)
        if count == 1:
            own[1] = dv
        else:
            parts[1, pl.ds(first, count)] = dv.astype(BF16).reshape(count, T, HEAD_SIZE)

    def key_part(key, first, count, dq_t):
        keys = kv[pl.ds(first, count), :, 0:HEAD_SIZE].reshape(count * T, HEAD_SIZE)
        values = kv[pl.ds(first, count), :, HEAD_SIZE:].reshape(count * T, HEAD_SIZE)
        low = probs[pl.ds(first, count)].reshape(count * T, N)
        dprob = dot(values, doc[place[key]], 1, 0)
        dscore = (low.astype(F32) * (dprob - deltas[key])).astype(BF16)
        dk = dot(dscore, qs[...], 1, 0) * SCALE
        if count == 1:
            own[0] = dk
        else:
            parts[0, pl.ds(first, count)] = dk.astype(BF16).reshape(count, T, HEAD_SIZE)
        return dq_t + dot(keys, dscore, 0, 0)

    def to_other_core(kv_of, kind):
        for yy in range(4):
            n = 4 * kind + yy
            send(parts.at[kv_of, slot(kind, yy, other)], sib.at[kv_of, n], SIB + 8 * kv_of + n, at(core=other))

    def along_y(kv_of, kind):
        for yy in range(4):
            n = 4 * kind + yy
            arrived(sib.at[kv_of, n], SIB + 8 * kv_of + n)
        for d in (1, 2, 3):
            yy = (y + d) % 4
            s = slot(kind, yy, c)
            parts[kv_of, s] = (parts[kv_of, s].astype(F32) + sib[kv_of, 4 * kind + yy].astype(F32)).astype(BF16)
            n = 6 * kv_of + 3 * kind + d - 1
            send(parts.at[kv_of, s], col.at[n], COL + n, at(dy=d))
        term = sib[kv_of, 4 * kind + y].astype(F32)
        if kind == 0:
            parts[kv_of, g1] = (parts[kv_of, g1].astype(F32) + term).astype(BF16)
        else:
            own[kv_of] += term * (1 - c).astype(F32)
            parts[kv_of, mix] = (parts[kv_of, mix].astype(F32) + term * c.astype(F32)).astype(BF16)

    def along_z(kv_of, kind):
        s = mix if kind == 1 else g1
        total = parts[kv_of, s].astype(F32)
        for d in (1, 2, 3):
            n = 6 * kv_of + 3 * kind + d - 1
            arrived(col.at[n], COL + n)
            term = col[n].astype(F32)
            if kind == 1:
                later = jnp.where(y - d < 0, 1.0, 0.0)
                own[kv_of] += term * later
                term = term * (1.0 - later)
            total = total + term
        parts[kv_of, s] = total.astype(BF16)
        n = 2 * kv_of + kind
        send(parts.at[kv_of, s], deep.at[n], DEEP + n, at(dh=-1 - kind))

    by_key = {key: (key, first, count) for key, first, count in chunks}
    for kind in (1, 0):
        value_part(*by_key[kind, 1])
        to_other_core(1, kind)
    value_part(*by_key["own"])
    for kind in (1, 0):
        value_part(*by_key[kind, 0])

    for n in range(7):
        arrived(rank_in.at[1 + n], RK + n)
    rank_sum = rank_in[0].astype(F32)
    for n in range(7):
        rank_sum = rank_sum + rank_in[1 + n].astype(F32)
    rank_acts = jnp.concatenate([rank_sum[:, :RANK], rank_sum[:, RANK:]], axis=0).astype(BF16)
    for g in range(GROUP):
        du[0:RANK, HEAD_SIZE * g : HEAD_SIZE * (g + 1)] = (
            GAIN * dot(rank_grad, out[T * g : T * (g + 1)], 0, 0)
        ).astype(BF16)
    du[RANK:, :] = (GAIN * dot(rank_acts, cots[mp], 0, 0)).astype(BF16)

    def piece(yy, cc):
        return pl.ds((yy * 2 + cc) * PIECE, PIECE)

    for n, (d, cc) in enumerate(plane):
        yy, core = (y + d) % 4, (c + cc) % 2
        send(du.at[piece(yy, core)], du_in.at[n], DU + n, at(dy=d, core=core))

    for kind in (1, 0):
        along_y(1, kind)
    dq_t = key_part(*by_key["own"], jnp.zeros((HEAD_SIZE, N), F32))
    for kind in (1, 0):
        dq_t = key_part(*by_key[kind, 1], dq_t)
        to_other_core(0, kind)

    total_du = du[piece(y, c)].astype(F32)
    for n in range(7):
        arrived(du_in.at[n], DU + n)
        total_du = total_du + du_in[n].astype(F32)
    du_z[3] = total_du.astype(BF16)
    for d in (1, 2, 3):
        send(du_z.at[3], du_z.at[d - 1], DU_Z + d - 1, at(dh=d))

    for kind in (1, 0):
        along_z(1, kind)
    for kind in (1, 0):
        dq_t = key_part(*by_key[kind, 0], dq_t)
        along_y(0, kind)

    for d in (1, 2, 3):
        arrived(du_z.at[d - 1], DU_Z + d - 1)
        total_du = total_du + du_z[d - 1].astype(F32)
    du_sum[piece(y, c)] = total_du.astype(BF16)
    for n, (d, cc) in enumerate(plane):
        send(du_sum.at[piece(y, c)], du_sum.at[piece(y, c)], DU_BACK + n, at(dy=d, core=(c + cc) % 2))

    results = []

    def store(src, dst):
        results.append(pltpu.make_async_copy(src, dst, load_sem.at[len(loads) + len(results)]))
        results[-1].start()

    for kind in (1, 0):
        along_z(0, kind)

    dq = (dq_t * SCALE).T.astype(BF16)
    for g in range(GROUP):
        dq_v[:, HEAD_SIZE * g : HEAD_SIZE * (g + 1)] = dq[T * g : T * (g + 1), :]
    store(dq_v, dq_out)

    for n, (d, cc) in enumerate(plane):
        arrived(du_sum.at[piece((y - d + 4) % 4, (c + cc) % 2)], DU_BACK + n)
    du_v[...] = du_sum[...].astype(F32)
    store(du_v.at[pl.ds(0, RANK)], down_out)
    store(du_v.at[pl.ds(RANK, RANK)], up_out)

    for kv_of, result in ((1, dv_out), (0, dk_out)):
        total = own[kv_of]
        for kind in (1, 0):
            arrived(deep.at[2 * kv_of + kind], DEEP + 2 * kv_of + kind)
            total = total + deep[2 * kv_of + kind].astype(F32)
        dkv_v[kv_of] = total.astype(BF16)
        store(dkv_v.at[kv_of], result)
    for copy in sent:
        copy.wait_send()
    for copy in results:
        copy.wait()


def hand_on(*refs):
    sources, results, held, sems = refs[0:5], refs[5:10], refs[10:15], refs[15]
    copies = [pltpu.make_async_copy(sources[n], held[n], sems.at[n]) for n in range(5)]
    for copy in copies:
        copy.start()
    outs = [pltpu.make_async_copy(held[n], results[n], sems.at[5 + n]) for n in range(5)]
    for n in (1, 2, 0, 3, 4):
        copies[n].wait()
        outs[n].start()
    for copy in outs:
        copy.wait()


def body(query_rows, key_rows, value_matrix, cotangent, frozen_out, adapter_down, adapter_up, doc_lengths):
    hbm = pl.BlockSpec(memory_space=pl.ANY)
    shapes = (
        jax.ShapeDtypeStruct((T, FEATURES), BF16),
        jax.ShapeDtypeStruct((T, HEAD_SIZE), BF16),
        jax.ShapeDtypeStruct((T, HEAD_SIZE), BF16),
        jax.ShapeDtypeStruct((RANK, FEATURES), F32),
        jax.ShapeDtypeStruct((RANK, FEATURES), F32),
    )
    outs = pl.pallas_call(
        kernel,
        out_shape=shapes,
        in_specs=[pl.BlockSpec(memory_space=pltpu.SMEM)] + [hbm] * 7,
        out_specs=(hbm,) * 5,
        scratch_shapes=[
            pltpu.VMEM((SLOTS, T, 2 * HEAD_SIZE), BF16),
            pltpu.VMEM((8, T, FEATURES), BF16),
            pltpu.VMEM((8, FEATURES + RANK, FEATURES), BF16),
            pltpu.VMEM((RANK, FEATURES), BF16),
            pltpu.VMEM((N, HEAD_SIZE), BF16),
            pltpu.VMEM((4, T, N), F32),
            pltpu.VMEM((SLOTS, T, N), BF16),
            pltpu.VMEM((N, HEAD_SIZE), F32),
            pltpu.VMEM((5, HEAD_SIZE, N), BF16),
            pltpu.VMEM((T, FEATURES + RANK), F32),
            pltpu.VMEM((2, 16, T, HEAD_SIZE), BF16),
            pltpu.VMEM((2, 8, T, HEAD_SIZE), BF16),
            pltpu.VMEM((12, T, HEAD_SIZE), BF16),
            pltpu.VMEM((4, T, HEAD_SIZE), BF16),
            pltpu.VMEM((2, T, HEAD_SIZE), F32),
            pltpu.VMEM((8, T // 2, 2 * RANK), BF16),
            pltpu.VMEM((2 * RANK, FEATURES), BF16),
            pltpu.VMEM((7, PIECE, FEATURES), BF16),
            pltpu.VMEM((4, PIECE, FEATURES), BF16),
            pltpu.VMEM((2 * RANK, FEATURES), BF16),
            pltpu.VMEM((T, FEATURES), BF16),
            pltpu.VMEM((2, T, HEAD_SIZE), BF16),
            pltpu.VMEM((2 * RANK, FEATURES), F32),
            pltpu.SemaphoreType.DMA((MESSAGES,)),
            pltpu.SemaphoreType.DMA((MESSAGES,)),
            pltpu.SemaphoreType.DMA((32,)),
        ],
        compiler_params=pltpu.CompilerParams(
            collective_id=0, has_side_effects=True, vmem_limit_bytes=60 * 2**20
        ),
    )(
        doc_lengths, query_rows, key_rows, value_matrix, cotangent,
        frozen_out, adapter_up, adapter_down.T,
    )
    dq, dk, dv, down_t, up = pl.pallas_call(
        hand_on,
        out_shape=shapes,
        in_specs=[hbm] * 5,
        out_specs=(hbm,) * 5,
        scratch_shapes=[pltpu.VMEM(shape.shape, shape.dtype) for shape in shapes]
        + [pltpu.SemaphoreType.DMA((10,))],
    )(*outs)
    return dq, dk, dv, down_t.T, up


def solution(mesh):
    return jax.shard_map(
        body,
        mesh=mesh,
        in_specs=(
            P("ctx", "mp"), P("ctx", "mp"), P("ctx", "mp"), P("ctx", "mp"), P("mp", None), P("mp", None), P(), P(),
        ),
        out_specs=(P("ctx", "mp"), P("ctx", "mp"), P("ctx", "mp"), P("mp", None), P(None, "mp")),
        check_vma=False,
    )
```

```python
import functools
import math

import jax
import jax.numpy as jnp
from jax import lax
from jax.experimental import pallas as pl
from jax.experimental.pallas import tpu as pltpu
from jax.sharding import PartitionSpec as P

HEAD_SIZE = 128
T = 160
GROUP = 5
N = 896
FEATURES = 640
RANK = 64
SLOTS = 17
SCALE = HEAD_SIZE**-0.5
EXP_SCALE = SCALE * math.log2(math.e)
GAIN = 2.0
MASKED = -1e30
MESH = pl.DeviceIdType.MESH
F32 = jnp.float32
BF16 = jnp.bfloat16
PIECE = 2 * RANK // 8

KV = 0
COT = 16
SIB = 30
COL = 46
DEEP = 58
RK = 62
DU = 69
DU_Z = 76
DU_BACK = 79
MESSAGES = 86


def dot(left, right, left_dim, right_dim):
    return lax.dot_general(
        left, right, (((left_dim,), (right_dim,)), ((), ())), preferred_element_type=F32
    )


def kernel(
    lengths, q_hbm, k_hbm, v_hbm, cot_hbm, w_hbm, up_hbm, down_hbm,
    dq_out, dk_out, dv_out, down_out, up_out,
    kv, cots, w, down, qs, scores, probs, dos, doc, acc, parts, sib, col, deep, own,
    rank_in, du, du_in, du_z, du_sum, dq_v, dkv_v, du_v, send_sem, recv_sem, load_sem,
):
    i = lax.axis_index("ctx")
    mp = lax.axis_index("mp")
    h, y, c = i // 8, (i // 2) % 4, i % 2
    x, zl = mp // 2, mp % 2
    other = 1 - c

    def at(dh=0, dy=0, core=None):
        return (
            ((h + dh + 4) % 4) * 8 + ((y + dy + 4) % 4) * 2 + (c if core is None else core),
            mp,
        )

    def along(dx=0, z=None):
        return (i, ((x + dx + 4) % 4) * 2 + (zl if z is None else z))

    def slot(kind, yy, cc):
        return kind * 8 + cc * 4 + yy

    sent = []

    def message_to(src, dst, message, device):
        copy = pltpu.make_async_remote_copy(
            src_ref=src, dst_ref=dst, send_sem=send_sem.at[len(sent)], recv_sem=recv_sem.at[message],
            device_id=device, device_id_type=MESH,
        )
        sent.append(copy)
        return copy

    def send(src, dst, message, device):
        message_to(src, dst, message, device).start()

    def arrived(dst, message):
        pltpu.make_async_remote_copy(
            src_ref=dst, dst_ref=dst, send_sem=send_sem.at[0], recv_sem=recv_sem.at[message],
            device_id=at(core=other), device_id_type=MESH,
        ).wait_recv()

    for kind in (0, 1):
        kv[slot(kind, y, c)] = jnp.zeros((T, 2 * HEAD_SIZE), BF16)
    barrier = pltpu.get_barrier_semaphore()
    plane = [(d, cc) for d in (0, 1, 2, 3) for cc in (0, 1) if (d, cc) != (0, 0)]
    ranks = [along(dx=d) for d in (1, 2, 3)] + [along(dx=d, z=1 - zl) for d in (0, 1, 2, 3)]
    partners = [at(dh=d) for d in (2, 1, 3)] + ranks + [at(dy=d, core=(c + cc) % 2) for d, cc in plane]
    for partner in partners:
        pl.semaphore_signal(barrier, inc=1, device_id=partner, device_id_type=MESH)

    loads = []

    def load(src, dst):
        loads.append(pltpu.make_async_copy(src, dst, load_sem.at[len(loads)]))
        loads[-1].start()

    load(k_hbm, kv.at[16, :, pl.ds(0, HEAD_SIZE)])
    load(v_hbm, kv.at[16, :, pl.ds(HEAD_SIZE, HEAD_SIZE)])
    load(cot_hbm, cots.at[mp])
    qs[T * GROUP : N, :] = jnp.zeros((N - T * GROUP, HEAD_SIZE), BF16)
    for copy in loads[0:3]:
        copy.wait()
    pl.semaphore_wait(barrier, len(partners))

    g1, mix = slot(0, y, c), slot(1, y, c)
    near = x * 2 + 1 - zl
    left, right, far = ((x + 3) % 4) * 2, ((x + 1) % 4) * 2, ((x + 2) % 4) * 2
    half0, half1 = pl.ds(0, T // 2), pl.ds(T // 2, T // 2)
    halves = (half0, half1)

    def half(block, n):
        return cots.at[block, halves[n]]

    limited = []

    def send_if(condition, src, dst, message, device):
        copy = message_to(src, dst, message, device)
        limited.append((condition, sent.pop()))
        sent.append(None)
        pl.when(condition)(copy.start)

    send_if(h < 3, kv.at[16], kv.at[g1], KV + g1, at(dh=1))
    send_if(h < 2, kv.at[16], kv.at[mix], KV + mix, at(dh=2))
    for n in (0, 1):
        send(half(mp, n), half(mp, n), COT + 2 + n, along(dx=1))
        send(half(mp, 1 - n), half(mp, 1 - n), COT + 5 - n, along(dx=-1))
    send(half(mp, 0), half(mp, 0), COT + 0, along(z=1 - zl))
    send(half(mp, 1), half(mp, 1), COT + 1, along(z=1 - zl))
    early, late = [], []
    for d in (1, 2, 3):
        copy = message_to(kv.at[16], kv.at[mix], KV + mix, at(dy=d))
        early.append((y + d < 4, copy))
        late.append((y + d >= 4, pltpu.make_async_remote_copy(
            src_ref=kv.at[mix], dst_ref=kv.at[mix], send_sem=send_sem.at[len(sent) - 1],
            recv_sem=recv_sem.at[KV + mix], device_id=at(dy=d), device_id_type=MESH)))
    copy = message_to(kv.at[16], kv.at[mix], KV + mix, at(core=other))
    early.append((c == 0, copy))
    late.append((c == 1, pltpu.make_async_remote_copy(
        src_ref=kv.at[mix], dst_ref=kv.at[mix], send_sem=send_sem.at[len(sent) - 1],
        recv_sem=recv_sem.at[KV + mix], device_id=at(core=other), device_id_type=MESH)))
    for condition, copy in early:
        pl.when(condition)(copy.start)

    for g in range(GROUP):
        load(q_hbm.at[:, pl.ds(HEAD_SIZE * g, HEAD_SIZE)], qs.at[pl.ds(T * g, T)])
    load(down_hbm, down)
    for b in range(8):
        load(w_hbm.at[:, pl.ds(FEATURES * b, FEATURES)], w.at[b, pl.ds(0, FEATURES)])
        load(up_hbm.at[:, pl.ds(FEATURES * b, FEATURES)], w.at[b, pl.ds(FEATURES, RANK)])

    token = lax.broadcasted_iota(jnp.int32, (1, N), 1)
    for g in range(GROUP):
        token = token - jnp.where(token >= T, T, 0)
    position = token + i * T
    end0 = lengths[0]
    end1 = end0 + lengths[1]
    end2 = end1 + lengths[2]
    start = jnp.where(
        position >= end2, end2, jnp.where(position >= end1, end1, jnp.where(position >= end0, end0, 0))
    )
    row = lax.broadcasted_iota(jnp.int32, (T, N), 0)

    def forward(first, count, bases, state, causal=False):
        keys = kv[pl.ds(first, count), :, 0:HEAD_SIZE].reshape(count * T, HEAD_SIZE)
        values = kv[pl.ds(first, count), :, HEAD_SIZE:].reshape(count * T, HEAD_SIZE)
        raw = dot(keys, qs[...], 1, 1).reshape(count, T, N)
        top = jnp.full((8, N), MASKED, F32)
        for s in range(count):
            allowed = row >= start - bases[s]
            if causal:
                allowed = allowed & (row <= token)
            block = jnp.where(allowed, raw[s], MASKED)
            scores[s] = block
            top = jnp.maximum(top, jnp.max(block.reshape(T // 8, 8, N), axis=0))
        peak = jnp.max(top, axis=0, keepdims=True) * EXP_SCALE
        if state is not None:
            peak = jnp.maximum(peak, state[0])
        weights = jnp.exp2(scores[0:count].reshape(count * T, N) * EXP_SCALE - peak)
        total = jnp.sum(weights.reshape(count * T // 8, 8, N), axis=0)
        low = weights.astype(BF16)
        probs[pl.ds(first, count)] = low.reshape(count, T, N)
        out_t = dot(values, low, 0, 0)
        if state is not None:
            decay = jnp.exp2(state[0] - peak)
            total = total + state[1] * decay
            out_t = out_t + state[2] * decay
        return peak, total, out_t

    def bases_of(kind, cc):
        out = []
        for yy in range(4):
            j = 2 * yy + cc
            if kind == 0:
                group = h - 1
            else:
                group = jnp.where(j < 2 * y + c, h, h - 2)
            out.append((8 * group + j) * T)
        return out

    def project(block):
        acc[...] += dot(cots[block], w[block], 1, 1)

    for copy in loads[3:8]:
        copy.wait()
    peaks = {}
    state = forward(16, 1, [i * T], None, causal=True)
    peaks["own"] = state[0]

    arrived(half(left + zl, 0), COT + 2)
    send(half(left + zl, 0), half(left + zl, 0), COT + 6, along(dx=1))
    arrived(half(right + zl, 1), COT + 5)
    send(half(right + zl, 1), half(right + zl, 1), COT + 7, along(dx=-1))
    pl.when(h >= 1)(lambda: arrived(kv.at[g1], KV + g1))
    for d in (1, 2, 3):
        send(kv.at[g1], kv.at[g1], KV + g1, at(dy=d))
    send(kv.at[g1], kv.at[g1], KV + g1, at(core=other))
    pl.when(h >= 2)(lambda: arrived(kv.at[mix], KV + mix))
    for condition, copy in late:
        pl.when(condition)(copy.start)
    arrived(half(near, 0), COT + 0)
    send(half(near, 0), half(near, 0), COT + 8, along(dx=1))
    arrived(half(near, 1), COT + 1)
    send(half(near, 1), half(near, 1), COT + 11, along(dx=-1))
    send(half(near, 1), half(near, 1), COT + 9, along(dx=1))
    send(half(near, 0), half(near, 0), COT + 10, along(dx=-1))
    for copy in loads[8:]:
        copy.wait()
    acc[...] = dot(cots[mp], w[mp], 1, 1)
    project(near)

    for kind in (0, 1):
        for d in (1, 2, 3):
            s = slot(kind, (y + d) % 4, c)
            arrived(kv.at[s], KV + s)
            send(kv.at[s], kv.at[s], KV + s, at(core=other))
        state = forward(slot(kind, 0, c), 4, bases_of(kind, c), state)
        peaks[kind, 0] = state[0]
        if kind == 0:
            arrived(half(left + 1 - zl, 0), COT + 8)
            send(half(left + 1 - zl, 0), half(left + 1 - zl, 0), COT + 12, along(dx=1))
            arrived(half(right + 1 - zl, 1), COT + 11)
            send(half(right + 1 - zl, 1), half(right + 1 - zl, 1), COT + 13, along(dx=-1))

    arrived(half(left + zl, 1), COT + 3)
    arrived(half(right + zl, 0), COT + 4)
    for block in (left + zl, right + zl):
        project(block)
    for kind in (0, 1):
        for yy in range(4):
            s = slot(kind, yy, other)
            arrived(kv.at[s], KV + s)
        state = forward(slot(kind, 0, other), 4, bases_of(kind, other), state)
        peaks[kind, 1] = state[0]

    peak, total, out_t = state
    inverse = 1.0 / jnp.sum(total, axis=0, keepdims=True)
    out_t = (out_t * inverse).astype(BF16).astype(F32)
    out = out_t.T.astype(BF16)

    rank_part = jnp.zeros((T, RANK), F32)
    for g in range(GROUP):
        rank_part = rank_part + dot(
            out[T * g : T * (g + 1)], down[:, HEAD_SIZE * g : HEAD_SIZE * (g + 1)], 1, 1
        )
    rank_in[0] = jnp.concatenate([rank_part[: T // 2], rank_part[T // 2 :]], axis=1).astype(BF16)
    for n, device in enumerate(ranks):
        send(rank_in.at[0], rank_in.at[1 + n], RK + n, device)

    arrived(half(left + 1 - zl, 1), COT + 9)
    project(left + 1 - zl)
    arrived(half(right + 1 - zl, 0), COT + 10)
    project(right + 1 - zl)
    arrived(half(far + zl, 0), COT + 6)
    arrived(half(far + zl, 1), COT + 7)
    project(far + zl)
    arrived(half(far + 1 - zl, 0), COT + 12)
    arrived(half(far + 1 - zl, 1), COT + 13)
    project(far + 1 - zl)
    rank_grad = acc[:, FEATURES:].astype(BF16)
    out_grad = (acc[:, 0:FEATURES] + GAIN * dot(rank_grad, down[...], 1, 0)).astype(BF16).astype(F32)
    for g in range(GROUP):
        dos[T * g : T * (g + 1), :] = out_grad[:, HEAD_SIZE * g : HEAD_SIZE * (g + 1)]
    dos[T * GROUP : N, :] = jnp.zeros((N - T * GROUP, HEAD_SIZE), F32)
    do_t = dos[...].T * inverse
    delta = jnp.sum(do_t * out_t, axis=0, keepdims=True)

    chunks = [("own", 16, 1)]
    chunks += [((kind, k), slot(kind, 0, c if k == 0 else other), 4) for k in (1, 0) for kind in (1, 0)]
    deltas, place = {}, {}
    for n, (key, first, count) in enumerate(chunks):
        factor = jnp.exp2(peaks[key] - peak)
        doc[n] = (do_t * factor).astype(BF16)
        deltas[key] = delta * factor
        place[key] = n

    def value_part(key, first, count):
        low = probs[pl.ds(first, count)].reshape(count * T, N)
        dv = dot(low, doc[place[key]], 1, 1)
        if count == 1:
            own[1] = dv
        else:
            parts[1, pl.ds(first, count)] = dv.astype(BF16).reshape(count, T, HEAD_SIZE)

    def key_part(key, first, count, dq_t):
        keys = kv[pl.ds(first, count), :, 0:HEAD_SIZE].reshape(count * T, HEAD_SIZE)
        values = kv[pl.ds(first, count), :, HEAD_SIZE:].reshape(count * T, HEAD_SIZE)
        low = probs[pl.ds(first, count)].reshape(count * T, N)
        dprob = dot(values, doc[place[key]], 1, 0)
        dscore = (low.astype(F32) * (dprob - deltas[key])).astype(BF16)
        dk = dot(dscore, qs[...], 1, 0) * SCALE
        if count == 1:
            own[0] = dk
        else:
            parts[0, pl.ds(first, count)] = dk.astype(BF16).reshape(count, T, HEAD_SIZE)
        return dq_t + dot(keys, dscore, 0, 0)

    def to_other_core(kv_of, kind):
        for yy in range(4):
            n = 4 * kind + yy
            send(parts.at[kv_of, slot(kind, yy, other)], sib.at[kv_of, n], SIB + 8 * kv_of + n, at(core=other))

    def along_y(kv_of, kind):
        for yy in range(4):
            n = 4 * kind + yy
            arrived(sib.at[kv_of, n], SIB + 8 * kv_of + n)
        for d in (1, 2, 3):
            yy = (y + d) % 4
            s = slot(kind, yy, c)
            parts[kv_of, s] = (parts[kv_of, s].astype(F32) + sib[kv_of, 4 * kind + yy].astype(F32)).astype(BF16)
            n = 6 * kv_of + 3 * kind + d - 1
            send(parts.at[kv_of, s], col.at[n], COL + n, at(dy=d))
        term = sib[kv_of, 4 * kind + y].astype(F32)
        if kind == 0:
            parts[kv_of, g1] = (parts[kv_of, g1].astype(F32) + term).astype(BF16)
        else:
            own[kv_of] += term * (1 - c).astype(F32)
            parts[kv_of, mix] = (parts[kv_of, mix].astype(F32) + term * c.astype(F32)).astype(BF16)

    def along_z(kv_of, kind):
        s = mix if kind == 1 else g1
        total = parts[kv_of, s].astype(F32)
        for d in (1, 2, 3):
            n = 6 * kv_of + 3 * kind + d - 1
            arrived(col.at[n], COL + n)
            term = col[n].astype(F32)
            if kind == 1:
                later = jnp.where(y - d < 0, 1.0, 0.0)
                own[kv_of] += term * later
                term = term * (1.0 - later)
            total = total + term
        parts[kv_of, s] = total.astype(BF16)
        n = 2 * kv_of + kind
        send_if(h >= 1 + kind, parts.at[kv_of, s], deep.at[n], DEEP + n, at(dh=-1 - kind))

    by_key = {key: (key, first, count) for key, first, count in chunks}
    for kind in (1, 0):
        value_part(*by_key[kind, 1])
        to_other_core(1, kind)
    value_part(*by_key["own"])
    for kind in (1, 0):
        value_part(*by_key[kind, 0])

    for n in range(7):
        arrived(rank_in.at[1 + n], RK + n)
    rank_sum = rank_in[0].astype(F32)
    for n in range(7):
        rank_sum = rank_sum + rank_in[1 + n].astype(F32)
    rank_acts = jnp.concatenate([rank_sum[:, :RANK], rank_sum[:, RANK:]], axis=0).astype(BF16)
    for g in range(GROUP):
        du[0:RANK, HEAD_SIZE * g : HEAD_SIZE * (g + 1)] = (
            GAIN * dot(rank_grad, out[T * g : T * (g + 1)], 0, 0)
        ).astype(BF16)
    du[RANK:, :] = (GAIN * dot(rank_acts, cots[mp], 0, 0)).astype(BF16)

    def piece(yy, cc):
        return pl.ds((yy * 2 + cc) * PIECE, PIECE)

    for n, (d, cc) in enumerate(plane):
        yy, core = (y + d) % 4, (c + cc) % 2
        send(du.at[piece(yy, core)], du_in.at[n], DU + n, at(dy=d, core=core))

    for kind in (1, 0):
        along_y(1, kind)
    dq_t = key_part(*by_key["own"], jnp.zeros((HEAD_SIZE, N), F32))
    for kind in (1, 0):
        dq_t = key_part(*by_key[kind, 1], dq_t)
        to_other_core(0, kind)

    total_du = du[piece(y, c)].astype(F32)
    for n in range(7):
        arrived(du_in.at[n], DU + n)
        total_du = total_du + du_in[n].astype(F32)
    du_z[3] = total_du.astype(BF16)
    for d in (1, 2, 3):
        send(du_z.at[3], du_z.at[d - 1], DU_Z + d - 1, at(dh=d))

    for kind in (1, 0):
        along_z(1, kind)
    for kind in (1, 0):
        dq_t = key_part(*by_key[kind, 0], dq_t)
        along_y(0, kind)

    for d in (1, 2, 3):
        arrived(du_z.at[d - 1], DU_Z + d - 1)
        total_du = total_du + du_z[d - 1].astype(F32)
    du_sum[piece(y, c)] = total_du.astype(BF16)
    for n, (d, cc) in enumerate(plane):
        send(du_sum.at[piece(y, c)], du_sum.at[piece(y, c)], DU_BACK + n, at(dy=d, core=(c + cc) % 2))

    results = []

    def store(src, dst):
        results.append(pltpu.make_async_copy(src, dst, load_sem.at[len(loads) + len(results)]))
        results[-1].start()

    for kind in (1, 0):
        along_z(0, kind)

    dq = (dq_t * SCALE).T.astype(BF16)
    for g in range(GROUP):
        dq_v[:, HEAD_SIZE * g : HEAD_SIZE * (g + 1)] = dq[T * g : T * (g + 1), :]
    store(dq_v, dq_out)

    for n, (d, cc) in enumerate(plane):
        arrived(du_sum.at[piece((y - d + 4) % 4, (c + cc) % 2)], DU_BACK + n)
    du_v[...] = du_sum[...].astype(F32)
    store(du_v.at[pl.ds(0, RANK)], down_out)
    store(du_v.at[pl.ds(RANK, RANK)], up_out)

    def add_deep(kv_of, kind):
        n = 2 * kv_of + kind
        arrived(deep.at[n], DEEP + n)
        own[kv_of] += deep[n].astype(F32)

    for kv_of, result in ((1, dv_out), (0, dk_out)):
        for kind in (1, 0):
            pl.when(h < 3 - kind)(functools.partial(add_deep, kv_of, kind))
        dkv_v[kv_of] = own[kv_of].astype(BF16)
        store(dkv_v.at[kv_of], result)
    for copy in sent:
        if copy is not None:
            copy.wait_send()
    for condition, copy in limited:
        pl.when(condition)(copy.wait_send)
    for copy in results:
        copy.wait()


def hand_on(*refs):
    sources, results, held, sems = refs[0:5], refs[5:10], refs[10:15], refs[15]
    copies = [pltpu.make_async_copy(sources[n], held[n], sems.at[n]) for n in range(5)]
    for copy in copies:
        copy.start()
    outs = [pltpu.make_async_copy(held[n], results[n], sems.at[5 + n]) for n in range(5)]
    for n in (1, 2, 0, 3, 4):
        copies[n].wait()
        outs[n].start()
    for copy in outs:
        copy.wait()


def body(query_rows, key_rows, value_matrix, cotangent, frozen_out, adapter_down, adapter_up, doc_lengths):
    hbm = pl.BlockSpec(memory_space=pl.ANY)
    shapes = (
        jax.ShapeDtypeStruct((T, FEATURES), BF16),
        jax.ShapeDtypeStruct((T, HEAD_SIZE), BF16),
        jax.ShapeDtypeStruct((T, HEAD_SIZE), BF16),
        jax.ShapeDtypeStruct((RANK, FEATURES), F32),
        jax.ShapeDtypeStruct((RANK, FEATURES), F32),
    )
    outs = pl.pallas_call(
        kernel,
        out_shape=shapes,
        in_specs=[pl.BlockSpec(memory_space=pltpu.SMEM)] + [hbm] * 7,
        out_specs=(hbm,) * 5,
        scratch_shapes=[
            pltpu.VMEM((SLOTS, T, 2 * HEAD_SIZE), BF16),
            pltpu.VMEM((8, T, FEATURES), BF16),
            pltpu.VMEM((8, FEATURES + RANK, FEATURES), BF16),
            pltpu.VMEM((RANK, FEATURES), BF16),
            pltpu.VMEM((N, HEAD_SIZE), BF16),
            pltpu.VMEM((4, T, N), F32),
            pltpu.VMEM((SLOTS, T, N), BF16),
            pltpu.VMEM((N, HEAD_SIZE), F32),
            pltpu.VMEM((5, HEAD_SIZE, N), BF16),
            pltpu.VMEM((T, FEATURES + RANK), F32),
            pltpu.VMEM((2, 16, T, HEAD_SIZE), BF16),
            pltpu.VMEM((2, 8, T, HEAD_SIZE), BF16),
            pltpu.VMEM((12, T, HEAD_SIZE), BF16),
            pltpu.VMEM((4, T, HEAD_SIZE), BF16),
            pltpu.VMEM((2, T, HEAD_SIZE), F32),
            pltpu.VMEM((8, T // 2, 2 * RANK), BF16),
            pltpu.VMEM((2 * RANK, FEATURES), BF16),
            pltpu.VMEM((7, PIECE, FEATURES), BF16),
            pltpu.VMEM((4, PIECE, FEATURES), BF16),
            pltpu.VMEM((2 * RANK, FEATURES), BF16),
            pltpu.VMEM((T, FEATURES), BF16),
            pltpu.VMEM((2, T, HEAD_SIZE), BF16),
            pltpu.VMEM((2 * RANK, FEATURES), F32),
            pltpu.SemaphoreType.DMA((MESSAGES,)),
            pltpu.SemaphoreType.DMA((MESSAGES,)),
            pltpu.SemaphoreType.DMA((32,)),
        ],
        compiler_params=pltpu.CompilerParams(
            collective_id=0, has_side_effects=True, vmem_limit_bytes=60 * 2**20
        ),
    )(
        doc_lengths, query_rows, key_rows, value_matrix, cotangent,
        frozen_out, adapter_up, adapter_down.T,
    )
    dq, dk, dv, down_t, up = pl.pallas_call(
        hand_on,
        out_shape=shapes,
        in_specs=[hbm] * 5,
        out_specs=(hbm,) * 5,
        scratch_shapes=[pltpu.VMEM(shape.shape, shape.dtype) for shape in shapes]
        + [pltpu.SemaphoreType.DMA((10,))],
    )(*outs)
    return dq, dk, dv, down_t.T, up


def solution(mesh):
    return jax.shard_map(
        body,
        mesh=mesh,
        in_specs=(
            P("ctx", "mp"), P("ctx", "mp"), P("ctx", "mp"), P("ctx", "mp"), P("mp", None), P("mp", None), P(), P(),
        ),
        out_specs=(P("ctx", "mp"), P("ctx", "mp"), P("ctx", "mp"), P("mp", None), P(None, "mp")),
        check_vma=False,
    )
```

```python
import functools
import math

import jax
import jax.numpy as jnp
from jax import lax
from jax.experimental import pallas as pl
from jax.experimental.pallas import tpu as pltpu
from jax.sharding import PartitionSpec as P

HEAD_SIZE = 128
T = 160
GROUP = 5
N = 896
FEATURES = 640
RANK = 64
SLOTS = 17
SCALE = HEAD_SIZE**-0.5
EXP_SCALE = SCALE * math.log2(math.e)
GAIN = 2.0
MASKED = -1e30
MESH = pl.DeviceIdType.MESH
F32 = jnp.float32
BF16 = jnp.bfloat16
PIECE = 2 * RANK // 8

KV = 0
COT = 16
SIB = 30
COL = 46
DEEP = 58
RK = 62
DU = 69
DU_Z = 76
DU_BACK = 79
MESSAGES = 86


def dot(left, right, left_dim, right_dim):
    return lax.dot_general(
        left, right, (((left_dim,), (right_dim,)), ((), ())), preferred_element_type=F32
    )


def kernel(
    lengths, q_hbm, k_hbm, v_hbm, cot_hbm, w_hbm, up_hbm, down_hbm,
    dq_out, dk_out, dv_out, down_out, up_out,
    kv, cots, w, down, qs, scores, probs, dos, doc, acc, parts, sib, col, deep, own,
    rank_in, du, du_in, du_z, du_sum, dq_v, dkv_v, du_v, send_sem, recv_sem, load_sem,
):
    i = lax.axis_index("ctx")
    mp = lax.axis_index("mp")
    h, y, c = i // 8, (i // 2) % 4, i % 2
    x, zl = mp // 2, mp % 2
    other = 1 - c

    def at(dh=0, dy=0, core=None):
        return (
            ((h + dh + 4) % 4) * 8 + ((y + dy + 4) % 4) * 2 + (c if core is None else core),
            mp,
        )

    def along(dx=0, z=None):
        return (i, ((x + dx + 4) % 4) * 2 + (zl if z is None else z))

    def slot(kind, yy, cc):
        return kind * 8 + cc * 4 + yy

    sent = []

    def message_to(src, dst, message, device):
        copy = pltpu.make_async_remote_copy(
            src_ref=src, dst_ref=dst, send_sem=send_sem.at[len(sent)], recv_sem=recv_sem.at[message],
            device_id=device, device_id_type=MESH,
        )
        sent.append(copy)
        return copy

    def send(src, dst, message, device):
        message_to(src, dst, message, device).start()

    def arrived(dst, message):
        pltpu.make_async_remote_copy(
            src_ref=dst, dst_ref=dst, send_sem=send_sem.at[0], recv_sem=recv_sem.at[message],
            device_id=at(core=other), device_id_type=MESH,
        ).wait_recv()

    for kind in (0, 1):
        kv[slot(kind, y, c)] = jnp.zeros((T, 2 * HEAD_SIZE), BF16)
    barrier = pltpu.get_barrier_semaphore()
    plane = [(d, cc) for d in (2, 1, 3, 0) for cc in (0, 1) if (d, cc) != (0, 0)]
    ranks = [along(dx=d) for d in (2, 1, 3)] + [along(dx=d, z=1 - zl) for d in (2, 1, 3, 0)]
    partners = [at(dh=d) for d in (2, 1, 3)] + ranks + [at(dy=d, core=(c + cc) % 2) for d, cc in plane]
    for partner in partners:
        pl.semaphore_signal(barrier, inc=1, device_id=partner, device_id_type=MESH)

    loads = []

    def load(src, dst):
        loads.append(pltpu.make_async_copy(src, dst, load_sem.at[len(loads)]))
        loads[-1].start()

    load(k_hbm, kv.at[16, :, pl.ds(0, HEAD_SIZE)])
    load(v_hbm, kv.at[16, :, pl.ds(HEAD_SIZE, HEAD_SIZE)])
    load(cot_hbm, cots.at[mp])
    qs[T * GROUP : N, :] = jnp.zeros((N - T * GROUP, HEAD_SIZE), BF16)
    for copy in loads[0:3]:
        copy.wait()
    pl.semaphore_wait(barrier, len(partners))

    g1, mix = slot(0, y, c), slot(1, y, c)
    near = x * 2 + 1 - zl
    left, right, far = ((x + 3) % 4) * 2, ((x + 1) % 4) * 2, ((x + 2) % 4) * 2
    half0, half1 = pl.ds(0, T // 2), pl.ds(T // 2, T // 2)
    halves = (half0, half1)

    def half(block, n):
        return cots.at[block, halves[n]]

    limited = []

    def send_if(condition, src, dst, message, device):
        copy = message_to(src, dst, message, device)
        limited.append((condition, sent.pop()))
        sent.append(None)
        pl.when(condition)(copy.start)

    send_if(h < 3, kv.at[16], kv.at[g1], KV + g1, at(dh=1))
    send_if(h < 2, kv.at[16], kv.at[mix], KV + mix, at(dh=2))
    for n in (0, 1):
        send(half(mp, n), half(mp, n), COT + 2 + n, along(dx=1))
        send(half(mp, 1 - n), half(mp, 1 - n), COT + 5 - n, along(dx=-1))
    send(half(mp, 0), half(mp, 0), COT + 0, along(z=1 - zl))
    send(half(mp, 1), half(mp, 1), COT + 1, along(z=1 - zl))
    early, late = [], []
    for d in (2, 1, 3):
        copy = message_to(kv.at[16], kv.at[mix], KV + mix, at(dy=d))
        early.append((y + d < 4, copy))
        late.append((y + d >= 4, pltpu.make_async_remote_copy(
            src_ref=kv.at[mix], dst_ref=kv.at[mix], send_sem=send_sem.at[len(sent) - 1],
            recv_sem=recv_sem.at[KV + mix], device_id=at(dy=d), device_id_type=MESH)))
    copy = message_to(kv.at[16], kv.at[mix], KV + mix, at(core=other))
    early.append((c == 0, copy))
    late.append((c == 1, pltpu.make_async_remote_copy(
        src_ref=kv.at[mix], dst_ref=kv.at[mix], send_sem=send_sem.at[len(sent) - 1],
        recv_sem=recv_sem.at[KV + mix], device_id=at(core=other), device_id_type=MESH)))
    for condition, copy in early:
        pl.when(condition)(copy.start)

    for g in range(GROUP):
        load(q_hbm.at[:, pl.ds(HEAD_SIZE * g, HEAD_SIZE)], qs.at[pl.ds(T * g, T)])
    load(down_hbm, down)
    for b in range(8):
        load(w_hbm.at[:, pl.ds(FEATURES * b, FEATURES)], w.at[b, pl.ds(0, FEATURES)])
        load(up_hbm.at[:, pl.ds(FEATURES * b, FEATURES)], w.at[b, pl.ds(FEATURES, RANK)])

    token = lax.broadcasted_iota(jnp.int32, (1, N), 1)
    for g in range(GROUP):
        token = token - jnp.where(token >= T, T, 0)
    position = token + i * T
    end0 = lengths[0]
    end1 = end0 + lengths[1]
    end2 = end1 + lengths[2]
    start = jnp.where(
        position >= end2, end2, jnp.where(position >= end1, end1, jnp.where(position >= end0, end0, 0))
    )
    row = lax.broadcasted_iota(jnp.int32, (T, N), 0)

    def forward(first, count, bases, state, causal=False):
        keys = kv[pl.ds(first, count), :, 0:HEAD_SIZE].reshape(count * T, HEAD_SIZE)
        values = kv[pl.ds(first, count), :, HEAD_SIZE:].reshape(count * T, HEAD_SIZE)
        raw = dot(keys, qs[...], 1, 1).reshape(count, T, N)
        top = jnp.full((8, N), MASKED, F32)
        for s in range(count):
            allowed = row >= start - bases[s]
            if causal:
                allowed = allowed & (row <= token)
            block = jnp.where(allowed, raw[s], MASKED)
            scores[s] = block
            top = jnp.maximum(top, jnp.max(block.reshape(T // 8, 8, N), axis=0))
        peak = jnp.max(top, axis=0, keepdims=True) * EXP_SCALE
        if state is not None:
            peak = jnp.maximum(peak, state[0])
        weights = jnp.exp2(scores[0:count].reshape(count * T, N) * EXP_SCALE - peak)
        total = jnp.sum(weights.reshape(count * T // 8, 8, N), axis=0)
        low = weights.astype(BF16)
        probs[pl.ds(first, count)] = low.reshape(count, T, N)
        out_t = dot(values, low, 0, 0)
        if state is not None:
            decay = jnp.exp2(state[0] - peak)
            total = total + state[1] * decay
            out_t = out_t + state[2] * decay
        return peak, total, out_t

    def bases_of(kind, cc):
        out = []
        for yy in range(4):
            j = 2 * yy + cc
            if kind == 0:
                group = h - 1
            else:
                group = jnp.where(j < 2 * y + c, h, h - 2)
            out.append((8 * group + j) * T)
        return out

    def project(block):
        acc[...] += dot(cots[block], w[block], 1, 1)

    for copy in loads[3:8]:
        copy.wait()
    peaks = {}
    state = forward(16, 1, [i * T], None, causal=True)
    peaks["own"] = state[0]

    arrived(half(left + zl, 0), COT + 2)
    send(half(left + zl, 0), half(left + zl, 0), COT + 6, along(dx=1))
    arrived(half(right + zl, 1), COT + 5)
    send(half(right + zl, 1), half(right + zl, 1), COT + 7, along(dx=-1))
    pl.when(h >= 1)(lambda: arrived(kv.at[g1], KV + g1))
    for d in (2, 1, 3):
        send(kv.at[g1], kv.at[g1], KV + g1, at(dy=d))
    send(kv.at[g1], kv.at[g1], KV + g1, at(core=other))
    pl.when(h >= 2)(lambda: arrived(kv.at[mix], KV + mix))
    for condition, copy in late:
        pl.when(condition)(copy.start)
    arrived(half(near, 0), COT + 0)
    send(half(near, 0), half(near, 0), COT + 8, along(dx=1))
    arrived(half(near, 1), COT + 1)
    send(half(near, 1), half(near, 1), COT + 11, along(dx=-1))
    send(half(near, 1), half(near, 1), COT + 9, along(dx=1))
    send(half(near, 0), half(near, 0), COT + 10, along(dx=-1))
    for copy in loads[8:]:
        copy.wait()
    acc[...] = dot(cots[mp], w[mp], 1, 1)
    project(near)

    for kind in (0, 1):
        for d in (2, 1, 3):
            s = slot(kind, (y + d) % 4, c)
            arrived(kv.at[s], KV + s)
            send(kv.at[s], kv.at[s], KV + s, at(core=other))
        state = forward(slot(kind, 0, c), 4, bases_of(kind, c), state)
        peaks[kind, 0] = state[0]
        if kind == 0:
            arrived(half(left + 1 - zl, 0), COT + 8)
            send(half(left + 1 - zl, 0), half(left + 1 - zl, 0), COT + 12, along(dx=1))
            arrived(half(right + 1 - zl, 1), COT + 11)
            send(half(right + 1 - zl, 1), half(right + 1 - zl, 1), COT + 13, along(dx=-1))

    arrived(half(left + zl, 1), COT + 3)
    arrived(half(right + zl, 0), COT + 4)
    for block in (left + zl, right + zl):
        project(block)
    for kind in (0, 1):
        for yy in range(4):
            s = slot(kind, yy, other)
            arrived(kv.at[s], KV + s)
        state = forward(slot(kind, 0, other), 4, bases_of(kind, other), state)
        peaks[kind, 1] = state[0]

    peak, total, out_t = state
    inverse = 1.0 / jnp.sum(total, axis=0, keepdims=True)
    out_t = (out_t * inverse).astype(BF16).astype(F32)
    out = out_t.T.astype(BF16)

    rank_part = jnp.zeros((T, RANK), F32)
    for g in range(GROUP):
        rank_part = rank_part + dot(
            out[T * g : T * (g + 1)], down[:, HEAD_SIZE * g : HEAD_SIZE * (g + 1)], 1, 1
        )
    rank_in[0] = jnp.concatenate([rank_part[: T // 2], rank_part[T // 2 :]], axis=1).astype(BF16)
    for n, device in enumerate(ranks):
        send(rank_in.at[0], rank_in.at[1 + n], RK + n, device)

    arrived(half(left + 1 - zl, 1), COT + 9)
    project(left + 1 - zl)
    arrived(half(right + 1 - zl, 0), COT + 10)
    project(right + 1 - zl)
    arrived(half(far + zl, 0), COT + 6)
    arrived(half(far + zl, 1), COT + 7)
    project(far + zl)
    arrived(half(far + 1 - zl, 0), COT + 12)
    arrived(half(far + 1 - zl, 1), COT + 13)
    project(far + 1 - zl)
    rank_grad = acc[:, FEATURES:].astype(BF16)
    out_grad = (acc[:, 0:FEATURES] + GAIN * dot(rank_grad, down[...], 1, 0)).astype(BF16).astype(F32)
    for g in range(GROUP):
        dos[T * g : T * (g + 1), :] = out_grad[:, HEAD_SIZE * g : HEAD_SIZE * (g + 1)]
    dos[T * GROUP : N, :] = jnp.zeros((N - T * GROUP, HEAD_SIZE), F32)
    do_t = dos[...].T * inverse
    delta = jnp.sum(do_t * out_t, axis=0, keepdims=True)

    chunks = [("own", 16, 1)]
    chunks += [((kind, k), slot(kind, 0, c if k == 0 else other), 4) for k in (1, 0) for kind in (1, 0)]
    deltas, place = {}, {}
    for n, (key, first, count) in enumerate(chunks):
        factor = jnp.exp2(peaks[key] - peak)
        doc[n] = (do_t * factor).astype(BF16)
        deltas[key] = delta * factor
        place[key] = n

    def value_part(key, first, count):
        low = probs[pl.ds(first, count)].reshape(count * T, N)
        dv = dot(low, doc[place[key]], 1, 1)
        if count == 1:
            own[1] = dv
        else:
            parts[1, pl.ds(first, count)] = dv.astype(BF16).reshape(count, T, HEAD_SIZE)

    def key_part(key, first, count, dq_t):
        keys = kv[pl.ds(first, count), :, 0:HEAD_SIZE].reshape(count * T, HEAD_SIZE)
        values = kv[pl.ds(first, count), :, HEAD_SIZE:].reshape(count * T, HEAD_SIZE)
        low = probs[pl.ds(first, count)].reshape(count * T, N)
        dprob = dot(values, doc[place[key]], 1, 0)
        dscore = (low.astype(F32) * (dprob - deltas[key])).astype(BF16)
        dk = dot(dscore, qs[...], 1, 0) * SCALE
        if count == 1:
            own[0] = dk
        else:
            parts[0, pl.ds(first, count)] = dk.astype(BF16).reshape(count, T, HEAD_SIZE)
        return dq_t + dot(keys, dscore, 0, 0)

    def to_other_core(kv_of, kind):
        for yy in range(4):
            n = 4 * kind + yy
            send(parts.at[kv_of, slot(kind, yy, other)], sib.at[kv_of, n], SIB + 8 * kv_of + n, at(core=other))

    def along_y(kv_of, kind):
        for yy in range(4):
            n = 4 * kind + yy
            arrived(sib.at[kv_of, n], SIB + 8 * kv_of + n)
        for d in (2, 1, 3):
            yy = (y + d) % 4
            s = slot(kind, yy, c)
            parts[kv_of, s] = (parts[kv_of, s].astype(F32) + sib[kv_of, 4 * kind + yy].astype(F32)).astype(BF16)
            n = 6 * kv_of + 3 * kind + d - 1
            send(parts.at[kv_of, s], col.at[n], COL + n, at(dy=d))
        term = sib[kv_of, 4 * kind + y].astype(F32)
        if kind == 0:
            parts[kv_of, g1] = (parts[kv_of, g1].astype(F32) + term).astype(BF16)
        else:
            own[kv_of] += term * (1 - c).astype(F32)
            parts[kv_of, mix] = (parts[kv_of, mix].astype(F32) + term * c.astype(F32)).astype(BF16)

    def along_z(kv_of, kind):
        s = mix if kind == 1 else g1
        total = parts[kv_of, s].astype(F32)
        for d in (2, 1, 3):
            n = 6 * kv_of + 3 * kind + d - 1
            arrived(col.at[n], COL + n)
            term = col[n].astype(F32)
            if kind == 1:
                later = jnp.where(y - d < 0, 1.0, 0.0)
                own[kv_of] += term * later
                term = term * (1.0 - later)
            total = total + term
        parts[kv_of, s] = total.astype(BF16)
        n = 2 * kv_of + kind
        send_if(h >= 1 + kind, parts.at[kv_of, s], deep.at[n], DEEP + n, at(dh=-1 - kind))

    by_key = {key: (key, first, count) for key, first, count in chunks}
    for kind in (1, 0):
        value_part(*by_key[kind, 1])
        to_other_core(1, kind)
    value_part(*by_key["own"])
    for kind in (1, 0):
        value_part(*by_key[kind, 0])

    for n in range(7):
        arrived(rank_in.at[1 + n], RK + n)
    rank_sum = rank_in[0].astype(F32)
    for n in range(7):
        rank_sum = rank_sum + rank_in[1 + n].astype(F32)
    rank_acts = jnp.concatenate([rank_sum[:, :RANK], rank_sum[:, RANK:]], axis=0).astype(BF16)
    for g in range(GROUP):
        du[0:RANK, HEAD_SIZE * g : HEAD_SIZE * (g + 1)] = (
            GAIN * dot(rank_grad, out[T * g : T * (g + 1)], 0, 0)
        ).astype(BF16)
    du[RANK:, :] = (GAIN * dot(rank_acts, cots[mp], 0, 0)).astype(BF16)

    def piece(yy, cc):
        return pl.ds((yy * 2 + cc) * PIECE, PIECE)

    for n, (d, cc) in enumerate(plane):
        yy, core = (y + d) % 4, (c + cc) % 2
        send(du.at[piece(yy, core)], du_in.at[n], DU + n, at(dy=d, core=core))

    for kind in (1, 0):
        along_y(1, kind)
    dq_t = key_part(*by_key["own"], jnp.zeros((HEAD_SIZE, N), F32))
    for kind in (1, 0):
        dq_t = key_part(*by_key[kind, 1], dq_t)
        to_other_core(0, kind)

    total_du = du[piece(y, c)].astype(F32)
    for n in range(7):
        arrived(du_in.at[n], DU + n)
        total_du = total_du + du_in[n].astype(F32)
    du_z[3] = total_du.astype(BF16)
    for d in (2, 1, 3):
        send(du_z.at[3], du_z.at[d - 1], DU_Z + d - 1, at(dh=d))

    for kind in (1, 0):
        along_z(1, kind)
    for kind in (1, 0):
        dq_t = key_part(*by_key[kind, 0], dq_t)
        along_y(0, kind)

    for d in (2, 1, 3):
        arrived(du_z.at[d - 1], DU_Z + d - 1)
        total_du = total_du + du_z[d - 1].astype(F32)
    du_sum[piece(y, c)] = total_du.astype(BF16)
    for n, (d, cc) in enumerate(plane):
        send(du_sum.at[piece(y, c)], du_sum.at[piece(y, c)], DU_BACK + n, at(dy=d, core=(c + cc) % 2))

    results = []

    def store(src, dst):
        results.append(pltpu.make_async_copy(src, dst, load_sem.at[len(loads) + len(results)]))
        results[-1].start()

    for kind in (1, 0):
        along_z(0, kind)

    dq = (dq_t * SCALE).T.astype(BF16)
    for g in range(GROUP):
        dq_v[:, HEAD_SIZE * g : HEAD_SIZE * (g + 1)] = dq[T * g : T * (g + 1), :]
    store(dq_v, dq_out)

    for n, (d, cc) in enumerate(plane):
        arrived(du_sum.at[piece((y - d + 4) % 4, (c + cc) % 2)], DU_BACK + n)
    du_v[...] = du_sum[...].astype(F32)
    store(du_v.at[pl.ds(0, RANK)], down_out)
    store(du_v.at[pl.ds(RANK, RANK)], up_out)

    def add_deep(kv_of, kind):
        n = 2 * kv_of + kind
        arrived(deep.at[n], DEEP + n)
        own[kv_of] += deep[n].astype(F32)

    for kv_of, result in ((1, dv_out), (0, dk_out)):
        for kind in (1, 0):
            pl.when(h < 3 - kind)(functools.partial(add_deep, kv_of, kind))
        dkv_v[kv_of] = own[kv_of].astype(BF16)
        store(dkv_v.at[kv_of], result)
    for copy in sent:
        if copy is not None:
            copy.wait_send()
    for condition, copy in limited:
        pl.when(condition)(copy.wait_send)
    for copy in results:
        copy.wait()


def hand_on(*refs):
    sources, results, held, sems = refs[0:5], refs[5:10], refs[10:15], refs[15]
    copies = [pltpu.make_async_copy(sources[n], held[n], sems.at[n]) for n in range(5)]
    for copy in copies:
        copy.start()
    outs = [pltpu.make_async_copy(held[n], results[n], sems.at[5 + n]) for n in range(5)]
    for n in (1, 2, 0, 3, 4):
        copies[n].wait()
        outs[n].start()
    for copy in outs:
        copy.wait()


def body(query_rows, key_rows, value_matrix, cotangent, frozen_out, adapter_down, adapter_up, doc_lengths):
    hbm = pl.BlockSpec(memory_space=pl.ANY)
    shapes = (
        jax.ShapeDtypeStruct((T, FEATURES), BF16),
        jax.ShapeDtypeStruct((T, HEAD_SIZE), BF16),
        jax.ShapeDtypeStruct((T, HEAD_SIZE), BF16),
        jax.ShapeDtypeStruct((RANK, FEATURES), F32),
        jax.ShapeDtypeStruct((RANK, FEATURES), F32),
    )
    outs = pl.pallas_call(
        kernel,
        out_shape=shapes,
        in_specs=[pl.BlockSpec(memory_space=pltpu.SMEM)] + [hbm] * 7,
        out_specs=(hbm,) * 5,
        scratch_shapes=[
            pltpu.VMEM((SLOTS, T, 2 * HEAD_SIZE), BF16),
            pltpu.VMEM((8, T, FEATURES), BF16),
            pltpu.VMEM((8, FEATURES + RANK, FEATURES), BF16),
            pltpu.VMEM((RANK, FEATURES), BF16),
            pltpu.VMEM((N, HEAD_SIZE), BF16),
            pltpu.VMEM((4, T, N), F32),
            pltpu.VMEM((SLOTS, T, N), BF16),
            pltpu.VMEM((N, HEAD_SIZE), F32),
            pltpu.VMEM((5, HEAD_SIZE, N), BF16),
            pltpu.VMEM((T, FEATURES + RANK), F32),
            pltpu.VMEM((2, 16, T, HEAD_SIZE), BF16),
            pltpu.VMEM((2, 8, T, HEAD_SIZE), BF16),
            pltpu.VMEM((12, T, HEAD_SIZE), BF16),
            pltpu.VMEM((4, T, HEAD_SIZE), BF16),
            pltpu.VMEM((2, T, HEAD_SIZE), F32),
            pltpu.VMEM((8, T // 2, 2 * RANK), BF16),
            pltpu.VMEM((2 * RANK, FEATURES), BF16),
            pltpu.VMEM((7, PIECE, FEATURES), BF16),
            pltpu.VMEM((4, PIECE, FEATURES), BF16),
            pltpu.VMEM((2 * RANK, FEATURES), BF16),
            pltpu.VMEM((T, FEATURES), BF16),
            pltpu.VMEM((2, T, HEAD_SIZE), BF16),
            pltpu.VMEM((2 * RANK, FEATURES), F32),
            pltpu.SemaphoreType.DMA((MESSAGES,)),
            pltpu.SemaphoreType.DMA((MESSAGES,)),
            pltpu.SemaphoreType.DMA((32,)),
        ],
        compiler_params=pltpu.CompilerParams(
            collective_id=0, has_side_effects=True, vmem_limit_bytes=60 * 2**20
        ),
    )(
        doc_lengths, query_rows, key_rows, value_matrix, cotangent,
        frozen_out, adapter_up, adapter_down.T,
    )
    dq, dk, dv, down_t, up = pl.pallas_call(
        hand_on,
        out_shape=shapes,
        in_specs=[hbm] * 5,
        out_specs=(hbm,) * 5,
        scratch_shapes=[pltpu.VMEM(shape.shape, shape.dtype) for shape in shapes]
        + [pltpu.SemaphoreType.DMA((10,))],
    )(*outs)
    return dq, dk, dv, down_t.T, up


def solution(mesh):
    return jax.shard_map(
        body,
        mesh=mesh,
        in_specs=(
            P("ctx", "mp"), P("ctx", "mp"), P("ctx", "mp"), P("ctx", "mp"), P("mp", None), P("mp", None), P(), P(),
        ),
        out_specs=(P("ctx", "mp"), P("ctx", "mp"), P("ctx", "mp"), P("mp", None), P(None, "mp")),
        check_vma=False,
    )
```
